128 devices in a mesh: prompt: 8 (over x, core), resp: 16 (over z, y).
Axes of the slice: x: 4, y: 4, z: 4, core: 2. Of those that a mesh axis runs over, the one named last changes fastest.
Arguments:
- queries: bfloat16 [128, 256, 4096], P(('prompt', 'resp')), may hold values from -5 to 5
- resp_keys: bfloat16 [128, 256, 512], P(('prompt', 'resp')), may hold values from -6 to 6
- resp_values: bfloat16 [128, 256, 512], P(('prompt', 'resp')), may hold values from -6 to 6
- grad_out: bfloat16 [128, 256, 4096], P(('prompt', 'resp')), may hold values from -24 to 24
- prompt_keys: bfloat16 [8, 256, 512], P('prompt', 'resp'), may hold values from -5 to 5
- prompt_values: bfloat16 [8, 256, 512], P('prompt', 'resp'), may hold values from -6 to 6
- group_sizes: int32 [8], replicated, may hold values from 1 to 64, 128 in all
- slot_response: int32 [128], replicated, may hold values from 0 to 127, each once
- lengths: int32 [128], P(('prompt', 'resp')), may hold values from 1 to 256, as said below
Outputs:
- grad_queries: bfloat16 [128, 256, 4096], P(('prompt', 'resp'))
- grad_resp_keys: bfloat16 [128, 256, 512], P(('prompt', 'resp'))
- grad_resp_values: bfloat16 [128, 256, 512], P(('prompt', 'resp'))
- grad_prompt_keys: float32 [8, 256, 512], P('prompt', 'resp')
- grad_prompt_values: float32 [8, 256, 512], P('prompt', 'resp')
The draws below stay inside these ranges and needn't reach their ends.
Inputs may be any that keep to these rules, and one draw needn't show every extreme that they name: `group_sizes`: group sizes sum to 128; a group may hold a single response; the largest is exactly 64. `slot_response`: each response appears in exactly one slot. `lengths`: some response block is full.
All inputs are finite; a program needn't handle non-finite values.
Results may differ from the reference program's by a relative error of at most 0.012.
Values may be sent and summed in bfloat16 or wider, within the bound.
No kernel may reach another device: no remote copies, remote signals or barrier semaphores. Data moves between devices by JAX's collectives and lax.ppermute only.
A program may use at most 128 MiB of HBM per device.

```python
import math
import jax
import jax.numpy as jnp
import numpy as np
from jax import lax

QH = 32
KVH = 4
HD = 128
TOK = 256
PL = 256
GRP = 8
QW = 4096
KVW = 512
NPROMPT = 8
RESP = 128
GMOST = 64


def draw_queries(key, part):
    key = jax.random.fold_in(key, 11)
    base = jnp.clip(jax.random.normal(key, (RESP, TOK, QW), jnp.float32), -5.0, 5.0)
    return base.astype(jnp.bfloat16)


def draw_prompt_keys(key, part):
    key = jax.random.fold_in(key, 12)
    base = jnp.clip(jax.random.normal(key, (NPROMPT, PL, KVW), jnp.float32), -5.0, 5.0)
    return base.astype(jnp.bfloat16)


def draw_lengths(key, part):
    key = jax.random.fold_in(key, 13)
    first_key, second_key = jax.random.split(key)
    values = jax.random.randint(first_key, (RESP,), 1, TOK + 1)
    full_at = jax.random.randint(second_key, (), 0, RESP)
    return jnp.where(jnp.arange(RESP) == full_at, TOK, values).astype(jnp.int32)


def levels(stream_key, extent, pieces, smallest, largest):
    factor_of = 1.0
    for dim, blocks in pieces:
        draws = jax.random.uniform(jax.random.fold_in(jax.random.fold_in(stream_key, 6), dim), (blocks,), jnp.float32, smallest / len(pieces), largest / len(pieces))
        factor_of = factor_of * jnp.repeat(jnp.exp(draws), extent[dim] // blocks).reshape((-1,) + (1,) * (len(extent) - 1 - dim))
    return factor_of


def length_profile(number_of, total, limit, slope):
    portions = [(1 << 20) // math.isqrt(standing ** slope) + 1 for standing in range(2, number_of + 1)]
    spare, holding = total - limit - (number_of - 1), [1] * (number_of - 1)
    while spare > 0:
        movable = [i for i in range(number_of - 1) if holding[i] < limit]
        whole, left = sum([portions[i] for i in movable]), spare
        for i in movable:
            addition = min(limit - holding[i], max(1, left * portions[i] // whole), spare)
            holding[i] = holding[i] + addition
            spare = spare - addition
    return np.array([limit] + holding)


def ragged(key, amount, total, bound, skew):
    if amount == 2:
        one = jax.random.randint(key, (), max(1, total - bound), min(bound, total - 1) + 1)
        return jnp.stack([one, total - one])
    sizes = jnp.asarray(length_profile(amount, total, bound, skew), jnp.int32)
    pairs = (amount - 1) // 2
    donor, sink = sizes[1:1 + 2 * pairs:2], sizes[2:2 + 2 * pairs:2]
    room = jnp.minimum(donor - 1, bound - sink)
    passed = jax.random.randint(jax.random.fold_in(key, 1), (pairs,), 0, 1 << 20) % (room + 1)
    sizes = sizes.at[1:1 + 2 * pairs:2].set(donor - passed).at[2:2 + 2 * pairs:2].set(sink + passed)
    return sizes[jax.random.permutation(jax.random.fold_in(key, 2), amount)]


def gaussian(key, shape, width, bound, shards=(), held_as=jnp.bfloat16):
    result = jax.random.normal(key, shape, jnp.float32) * width
    if len(shards) > 0:
        result = levels(key, shape, shards, -0.22, 0.18) * result
    return jnp.clip(result, min=-bound, max=bound).astype(held_as)


def setup_inputs(seed: int = 0) -> dict:
    arg_keys = jax.random.split(jax.random.key(seed), 10)
    return {
        "queries": draw_queries(jax.random.fold_in(arg_keys[9], 71), 0),
        "resp_keys": gaussian(arg_keys[1], (RESP, TOK, KVW), 1.0, 6.0, ((0, 128),)),
        "resp_values": gaussian(arg_keys[2], (RESP, TOK, KVW), 1.0, 6.0, ((0, 128),)),
        "grad_out": gaussian(arg_keys[3], (RESP, TOK, QW), 4.0, 24.0, ((0, 128),)),
        "prompt_keys": draw_prompt_keys(jax.random.fold_in(arg_keys[9], 71), 0),
        "prompt_values": gaussian(arg_keys[5], (NPROMPT, PL, KVW), 1.0, 6.0, ((0, 8), (1, 16))),
        "group_sizes": ragged(arg_keys[6], NPROMPT, RESP, GMOST, 2).astype(jnp.int32),
        "slot_response": jax.random.permutation(arg_keys[7], RESP).astype(jnp.int32),
        "lengths": draw_lengths(jax.random.fold_in(arg_keys[9], 71), 0),
    }


def per_response(query, prompt_k, prompt_v, resp_k, resp_v, upstream, length):
    tok_count = query.shape[0]
    prompt_len = prompt_k.shape[0]
    scaling = 1.0 / math.sqrt(HD)
    key_rows = jnp.concatenate([prompt_k, resp_k], 0).astype(jnp.float32).reshape(-1, KVH, HD)
    value_rows = jnp.concatenate([prompt_v, resp_v], 0).astype(jnp.float32).reshape(-1, KVH, HD)
    row_ids = jnp.arange(tok_count)[:, None]
    col_ids = jnp.arange(prompt_len + tok_count)[None, :] - prompt_len
    allowed = (col_ids < 0) | (col_ids <= row_ids) & (col_ids < length)
    live_rows = jnp.arange(tok_count) < length
    upstream = jnp.where(live_rows[:, None], upstream, jnp.zeros_like(upstream))
    query_f = query.astype(jnp.float32).reshape(tok_count, KVH, GRP, HD)
    upstream_f = upstream.astype(jnp.float32).reshape(tok_count, KVH, GRP, HD)
    scores = jnp.einsum('tkgh,jkh->kgtj', query_f, key_rows) * scaling
    scores = jnp.where(allowed[None, None], scores, -jnp.inf)
    row_max = lax.optimization_barrier(jnp.max(scores, axis=-1, keepdims=True))
    unnorm = jnp.exp(scores - row_max)
    probs = unnorm / lax.optimization_barrier(jnp.sum(unnorm, axis=-1, keepdims=True))
    probs_low = lax.optimization_barrier(probs.astype(jnp.bfloat16)).astype(jnp.float32)
    attended = jnp.einsum('kgtj,jkh->tkgh', probs_low, value_rows)
    row_dot = lax.optimization_barrier(jnp.sum(upstream_f * attended, axis=-1))
    dprob = jnp.einsum('tkgh,jkh->kgtj', upstream_f, value_rows)
    dscore = probs * (dprob - jnp.transpose(row_dot, (1, 2, 0))[..., None])
    dscore = lax.optimization_barrier(dscore.astype(jnp.bfloat16)).astype(jnp.float32)
    grad_q = jnp.einsum('kgtj,jkh->tkgh', dscore, key_rows) * scaling
    grad_k = jnp.einsum('kgtj,tkgh->jkh', dscore, query_f) * scaling
    grad_v = jnp.einsum('kgtj,tkgh->jkh', probs_low, upstream_f)
    grad_k = grad_k.reshape(prompt_len + tok_count, KVH * HD)
    grad_v = grad_v.reshape(prompt_len + tok_count, KVH * HD)
    grad_q = grad_q.reshape(tok_count, QH * HD).astype(jnp.bfloat16)
    return (grad_q, grad_k[:prompt_len], grad_v[:prompt_len], grad_k[prompt_len:].astype(jnp.bfloat16), grad_v[prompt_len:].astype(jnp.bfloat16))

def reference(queries, resp_keys, resp_values, grad_out, prompt_keys, prompt_values, group_sizes, slot_response, lengths):
    group_ends = jnp.cumsum(group_sizes)
    prompt_of = lax.optimization_barrier(jnp.sum((slot_response[:, None] >= group_ends[None, :]).astype(jnp.int32), axis=1)).astype(jnp.int32)

    def apply_one(packed):
        query, resp_k, resp_v, upstream, prompt_id, length = packed
        return per_response(query, prompt_keys[prompt_id], prompt_values[prompt_id], resp_k, resp_v, upstream, length)
    grad_q, prompt_kg, prompt_vg, resp_kg, resp_vg = lax.map(apply_one, (queries, resp_keys, resp_values, grad_out, prompt_of, lengths))
    grad_pk = jnp.zeros(prompt_keys.shape, jnp.float32).at[prompt_of].add(prompt_kg)
    grad_pv = jnp.zeros(prompt_values.shape, jnp.float32).at[prompt_of].add(prompt_vg)
    return (grad_q, resp_kg, resp_vg, grad_pk, grad_pv)
```

```python
import functools
import math

import jax
import jax.numpy as jnp
from jax import lax
from jax.experimental import pallas as pl
from jax.experimental.pallas import tpu as pltpu
from jax.sharding import PartitionSpec as P

KVH = 4
HD = 128
GRP = 8
TOK = 256
HALF = 128
PL = 256
ROWS = 16
NPROMPT = 8
SCALING = 1.0 / math.sqrt(HD)
EXP2_SCALE = SCALING * math.log2(math.e)
BF16 = jnp.bfloat16
F32 = jnp.float32


def contract_last(a, b):
    return lax.dot_general(a, b, (((1,), (1,)), ((), ())), preferred_element_type=F32)


def prompt_index(sizes_ref, slot):
    found = jnp.int32(0)
    end = jnp.int32(0)
    for p in range(NPROMPT - 1):
        end = end + sizes_ref[p]
        found = found + (slot >= end).astype(jnp.int32)
    return found


def split_kernel(keys_ref, values_ref, out_ref):
    for k in range(KVH):
        out_ref[k] = keys_ref[0, :, k * HD : (k + 1) * HD]
        out_ref[KVH + k] = values_ref[0, :, k * HD : (k + 1) * HD]


def select_kernel(sizes_ref, slots_ref, blocks_ref, out_ref):
    def body(d, carry):
        out_ref[d] = blocks_ref[prompt_index(sizes_ref, slots_ref[d])]
        return carry

    lax.fori_loop(0, out_ref.shape[0], body, 0, unroll=8)


def sum_kernel(sizes_ref, slots_ref, terms_ref, out_ref):
    out_ref[...] = jnp.zeros_like(out_ref)

    def body(d, carry):
        p = prompt_index(sizes_ref, slots_ref[d])
        out_ref[p] += terms_ref[d].astype(F32)
        return carry

    lax.fori_loop(0, terms_ref.shape[0], body, 0, unroll=8)


def join_kernel(blocks_ref, keys_ref, values_ref):
    for k in range(KVH):
        keys_ref[0, :, k * HD : (k + 1) * HD] = blocks_ref[k]
        values_ref[0, :, k * HD : (k + 1) * HD] = blocks_ref[KVH + k]


def attend_kernel(
    length_ref, q_ref, do_ref, kr_ref, vr_ref, kp_ref, vp_ref,
    dq_ref, dkr_ref, dvr_ref, dp_ref, dk_acc, dv_acc,
):
    length = length_ref[0]
    keys = jnp.concatenate([kp_ref[0], kr_ref[0]], axis=0)
    values = jnp.concatenate([vp_ref[0], vr_ref[0]], axis=0)
    keys_t = jnp.transpose(keys)
    lane = lax.broadcasted_iota(jnp.int32, (1, 2 * HALF), 1) % HALF
    causal = lax.broadcasted_iota(jnp.int32, (HALF, 2 * HALF), 0) <= lane
    dk_acc[...] = jnp.zeros_like(dk_acc)
    dv_acc[...] = jnp.zeros_like(dv_acc)

    def unit(pair, upper):
        count = PL + HALF * (1 + upper)
        rows = pl.ds(upper * HALF, HALF)
        first = pl.ds(pl.multiple_of(pair * (2 * HD), 2 * HD), HD)
        second = pl.ds(pl.multiple_of(pair * (2 * HD) + HD, HD), HD)
        q = jnp.concatenate([q_ref[0, rows, first], q_ref[0, rows, second]], axis=0)
        do = jnp.concatenate([do_ref[0, rows, first], do_ref[0, rows, second]], axis=0)
        s = contract_last(keys[:count], q)
        s = jnp.concatenate(
            [s[: count - HALF], jnp.where(causal, s[count - HALF :], -1e30)], axis=0
        )
        m = jnp.max(s, axis=0, keepdims=True)
        e = jnp.exp2(s * EXP2_SCALE - m * EXP2_SCALE)
        d = contract_last(values[:count], do)
        total = jnp.sum(e, axis=0, keepdims=True)
        inv = 1.0 / total
        r = jnp.sum(e * d, axis=0, keepdims=True) * inv
        live = lane + upper * HALF < length
        p = e * jnp.where(live, inv, 0.0)
        ds = (p * (d - r)).astype(BF16)
        dv_acc[:count] += jnp.dot(p.astype(BF16), do, preferred_element_type=F32)
        dk_acc[:count] += jnp.dot(ds, q, preferred_element_type=F32)
        dq_t = jnp.dot(keys_t[:, :count], ds, preferred_element_type=F32)
        dq = (jnp.transpose(dq_t) * SCALING).astype(BF16)
        dq_ref[0, rows, first] = dq[:HALF]
        dq_ref[0, rows, second] = dq[HALF:]

    for pair in range(GRP // 2):
        unit(pair, 0)
        unit(pair, 1)
    dk = dk_acc[...] * SCALING
    dv = dv_acc[...]
    dkr_ref[0] = dk[PL:].astype(BF16)
    dvr_ref[0] = dv[PL:].astype(BF16)
    dp_ref[0, 0] = dk[:PL].astype(BF16)
    dp_ref[1, 0] = dv[:PL].astype(BF16)


def attend(queries, resp_keys, resp_values, grad_out, prompt_kv, lengths):
    wide = pl.BlockSpec((1, TOK, GRP * HD), lambda k: (0, 0, k))
    narrow = pl.BlockSpec((1, TOK, HD), lambda k: (0, 0, k))
    return pl.pallas_call(
        attend_kernel,
        grid=(KVH,),
        in_specs=[
            pl.BlockSpec(memory_space=pltpu.SMEM),
            wide,
            wide,
            narrow,
            narrow,
            pl.BlockSpec((1, PL, HD), lambda k: (k, 0, 0)),
            pl.BlockSpec((1, PL, HD), lambda k: (KVH + k, 0, 0)),
        ],
        out_specs=[
            wide,
            narrow,
            narrow,
            pl.BlockSpec((2, 1, PL, HD), lambda k: (0, k, 0, 0)),
        ],
        out_shape=[
            jax.ShapeDtypeStruct(queries.shape, BF16),
            jax.ShapeDtypeStruct(resp_keys.shape, BF16),
            jax.ShapeDtypeStruct(resp_values.shape, BF16),
            jax.ShapeDtypeStruct((2, KVH, PL, HD), BF16),
        ],
        scratch_shapes=[pltpu.VMEM((PL + TOK, HD), F32), pltpu.VMEM((PL + TOK, HD), F32)],
        compiler_params=pltpu.CompilerParams(vmem_limit_bytes=48 * 1024 * 1024),
        cost_estimate=pl.CostEstimate(
            flops=5 * 2 * 8192 * 448 * 128, bytes_accessed=8 << 20, transcendentals=8192 * 448
        ),
        name="attend",
    )(lengths, queries, grad_out, resp_keys, resp_values, prompt_kv, prompt_kv)


def in_smem():
    return pl.BlockSpec(memory_space=pltpu.SMEM)


def in_vmem():
    return pl.BlockSpec(memory_space=pltpu.VMEM)


def per_device(
    queries,
    resp_keys,
    resp_values,
    grad_out,
    prompt_keys,
    prompt_values,
    group_sizes,
    slot_response,
    lengths,
):
    slots = slot_response.shape[0]
    split = pl.pallas_call(
        split_kernel,
        in_specs=[in_vmem(), in_vmem()],
        out_specs=in_vmem(),
        out_shape=jax.ShapeDtypeStruct((2 * KVH, ROWS, HD), BF16),
        name="split",
    )(prompt_keys, prompt_values)
    every = lax.all_to_all(split, "prompt", 0, 0)
    chosen = pl.pallas_call(
        select_kernel,
        in_specs=[in_smem(), in_smem(), in_vmem()],
        out_specs=in_vmem(),
        out_shape=jax.ShapeDtypeStruct((slots, ROWS, HD), BF16),
        name="select",
    )(group_sizes, slot_response, every)
    own = lax.all_to_all(chosen, ("prompt", "resp"), 0, 0)
    grad_q, grad_rk, grad_rv, grad_p = attend(
        queries, resp_keys, resp_values, grad_out, own.reshape(2 * KVH, PL, HD), lengths
    )
    terms = lax.all_to_all(grad_p.reshape(slots, ROWS, HD), ("prompt", "resp"), 0, 0)
    sums = pl.pallas_call(
        sum_kernel,
        in_specs=[in_smem(), in_smem(), in_vmem()],
        out_specs=in_vmem(),
        out_shape=jax.ShapeDtypeStruct((NPROMPT, ROWS, HD), F32),
        name="sum_terms",
    )(group_sizes, slot_response, terms)
    owned = lax.all_to_all(sums, "prompt", 0, 0)
    grad_pk, grad_pv = pl.pallas_call(
        join_kernel,
        in_specs=[in_vmem()],
        out_specs=[in_vmem(), in_vmem()],
        out_shape=[
            jax.ShapeDtypeStruct(prompt_keys.shape, F32),
            jax.ShapeDtypeStruct(prompt_values.shape, F32),
        ],
        name="join",
    )(owned)
    return (grad_q, grad_rk, grad_rv, grad_pk, grad_pv)


def solution(mesh):
    slot = ("prompt", "resp")
    in_specs = (
        P(slot, None, None),
        P(slot, None, None),
        P(slot, None, None),
        P(slot, None, None),
        P("prompt", "resp", None),
        P("prompt", "resp", None),
        P(),
        P(),
        P(slot),
    )
    out_specs = (
        P(slot, None, None),
        P(slot, None, None),
        P(slot, None, None),
        P("prompt", "resp", None),
        P("prompt", "resp", None),
    )
    return jax.shard_map(
        per_device, mesh=mesh, in_specs=in_specs, out_specs=out_specs, check_vma=False
    )
```

```python
import math

import jax
import jax.numpy as jnp
from jax import lax
from jax.experimental import pallas as pl
from jax.experimental.pallas import tpu as pltpu
from jax.sharding import PartitionSpec as P

KVH = 4
HD = 128
GRP = 8
TOK = 256
HALF = 128
PL = 256
ROWS = 16
KVW = KVH * HD
NPROMPT = 8
PAIRS = GRP // 2
UNITS = 2 * PAIRS
LANES = 2 * HALF
SCALING = 1.0 / math.sqrt(HD)
EXP2_SCALE = SCALING * math.log2(math.e)
BF16 = jnp.bfloat16
F32 = jnp.float32
VMEM_LIMIT = 60 * 1024 * 1024
BOTH = ("prompt", "resp")


def contract_last(a, b):
    return lax.dot_general(a, b, (((1,), (1,)), ((), ())), preferred_element_type=F32)


def matmul(a, b):
    return jnp.dot(a, b, preferred_element_type=F32)


def index_kernel(sizes_ref, slots_ref, first_ref, out_ref):
    def body(j, carry):
        slot = slots_ref[first_ref[0] + j]
        found = jnp.int32(0)
        end = jnp.int32(0)
        for p in range(NPROMPT - 1):
            end = end + sizes_ref[p]
            found = found + (slot >= end).astype(jnp.int32)
        out_ref[j] = found
        return carry

    lax.fori_loop(0, out_ref.shape[0], body, 0)


def spread_kernel(keys_ref, values_ref, out_ref):
    for i in range(NPROMPT):
        out_ref[i] = (keys_ref if i % 2 == 0 else values_ref)[0]


def select_kernel(index_ref, blocks_ref, out_ref):
    for j in range(out_ref.shape[0]):
        out_ref[j] = blocks_ref[index_ref[j]]


def sum_kernel(index_ref, terms_ref, out_ref):
    out_ref[...] = jnp.zeros_like(out_ref)
    for j in range(terms_ref.shape[0]):
        out_ref[index_ref[j]] += terms_ref[j].astype(F32)


def join_kernel(blocks_ref, keys_ref, values_ref):
    keys_ref[0] = (blocks_ref[0] + blocks_ref[2]) + (blocks_ref[4] + blocks_ref[6])
    values_ref[0] = (blocks_ref[1] + blocks_ref[3]) + (blocks_ref[5] + blocks_ref[7])


def unit_rows(ref, pair, upper):
    rows = slice(upper * HALF, (upper + 1) * HALF)
    at = pair * 2 * HD
    return jnp.concatenate(
        [ref[0, rows, at : at + HD], ref[0, rows, at + HD : at + 2 * HD]], axis=0
    )


def all_rows(ref):
    return jnp.concatenate(
        [unit_rows(ref, pair, upper) for upper in range(2) for pair in range(PAIRS)], axis=0
    )


def resp_scores(kr, q, upper):
    count = HALF * (1 + upper)
    s = contract_last(kr[:count], q)
    lane = lax.broadcasted_iota(jnp.int32, (HALF, LANES), 1) % HALF
    causal = lax.broadcasted_iota(jnp.int32, (HALF, LANES), 0) <= lane
    last = jnp.where(causal, s[count - HALF :], -1e30)
    if upper:
        return jnp.concatenate([s[:HALF], last], axis=0)
    return last


def resp_stats_kernel(q_ref, do_ref, kr_ref, vr_ref, stats_ref):
    kr = kr_ref[0]
    vr = vr_ref[0]
    for upper in range(2):
        for pair in range(PAIRS):
            q = unit_rows(q_ref, pair, upper)
            do = unit_rows(do_ref, pair, upper)
            s = resp_scores(kr, q, upper)
            d = contract_last(vr[: HALF * (1 + upper)], do)
            m = jnp.max(s, axis=0, keepdims=True)
            e = jnp.exp2(s * EXP2_SCALE - m * EXP2_SCALE)
            total = jnp.sum(e, axis=0, keepdims=True)
            weighted = jnp.sum(e * d, axis=0, keepdims=True)
            unit = upper * PAIRS + pair
            stats_ref[0, unit, 0:1] = m
            stats_ref[0, unit, 1:2] = total
            stats_ref[0, unit, 2:3] = weighted


def prompt_kernel(
    length_ref, q_ref, do_ref, kp_ref, vp_ref, stats_ref, grad_ref, ds_ref, final_ref, p_ref
):
    length = length_ref[0]
    kp = kp_ref[...]
    vp = vp_ref[...]
    lane = lax.broadcasted_iota(jnp.int32, (1, LANES), 1) % HALF
    for upper in range(2):
        for pair in range(PAIRS):
            unit = upper * PAIRS + pair
            q = unit_rows(q_ref, pair, upper)
            do = unit_rows(do_ref, pair, upper)
            s = contract_last(kp, q)
            d = contract_last(vp, do)
            resp_m = stats_ref[0, unit, 0:1]
            m = jnp.maximum(jnp.max(s, axis=0, keepdims=True), resp_m)
            e = jnp.exp2(s * EXP2_SCALE - m * EXP2_SCALE)
            fade = jnp.exp2((resp_m - m) * EXP2_SCALE)
            total = jnp.sum(e, axis=0, keepdims=True) + fade * stats_ref[0, unit, 1:2]
            weighted = jnp.sum(e * d, axis=0, keepdims=True) + fade * stats_ref[0, unit, 2:3]
            inv = 1.0 / total
            r = weighted * inv
            inv = jnp.where(lane + upper * HALF < length, inv, 0.0)
            p = e * inv
            cols = slice(unit * LANES, (unit + 1) * LANES)
            ds_ref[0, :, cols] = (p * (d - r)).astype(BF16)
            p_ref[:, cols] = p.astype(BF16)
            final_ref[0, unit, 0:1] = m
            final_ref[0, unit, 1:2] = inv
            final_ref[0, unit, 2:3] = r
    grad_ref[0] = (matmul(ds_ref[0], all_rows(q_ref)) * SCALING).astype(BF16)
    grad_ref[1] = matmul(p_ref[...], all_rows(do_ref)).astype(BF16)


def resp_kernel(*refs):
    q_ref, do_ref, kr_ref, vr_ref, kp_ref, ds_ref, final_ref = refs[:7]
    dq_ref, dkr_ref, dvr_ref, dsr_ref, p_ref = refs[-5:]
    kr = kr_ref[0]
    vr = vr_ref[0]
    keys_t = jnp.transpose(jnp.concatenate([kp_ref[...], kr], axis=0))
    for upper in range(2):
        count = HALF * (1 + upper)
        for pair in range(PAIRS):
            unit = upper * PAIRS + pair
            q = unit_rows(q_ref, pair, upper)
            do = unit_rows(do_ref, pair, upper)
            s = resp_scores(kr, q, upper)
            d = contract_last(vr[:count], do)
            m = final_ref[0, unit, 0:1]
            inv = final_ref[0, unit, 1:2]
            r = final_ref[0, unit, 2:3]
            p = jnp.exp2(s * EXP2_SCALE - m * EXP2_SCALE) * inv
            ds = (p * (d - r)).astype(BF16)
            cols = slice(unit * LANES, (unit + 1) * LANES)
            dsr_ref[:count, cols] = ds
            p_ref[:count, cols] = p.astype(BF16)
            both = jnp.concatenate([ds_ref[0, :, cols], ds], axis=0)
            dq = (jnp.transpose(matmul(keys_t[:, : PL + count], both)) * SCALING).astype(BF16)
            rows = slice(upper * HALF, (upper + 1) * HALF)
            at = pair * 2 * HD
            dq_ref[0, rows, at : at + HD] = dq[:HALF]
            dq_ref[0, rows, at + HD : at + 2 * HD] = dq[HALF:]
    for out_ref, left_ref, right_ref, scale in (
        (dkr_ref, dsr_ref, q_ref, SCALING),
        (dvr_ref, p_ref, do_ref, 1.0),
    ):
        right = all_rows(right_ref)
        split = PAIRS * LANES
        out_ref[0, :HALF] = (matmul(left_ref[:HALF], right) * scale).astype(BF16)
        out_ref[0, HALF:] = (matmul(left_ref[HALF:, split:], right[split:]) * scale).astype(BF16)


def in_smem():
    return pl.BlockSpec(memory_space=pltpu.SMEM)


def in_vmem():
    return pl.BlockSpec(memory_space=pltpu.VMEM)


def shape_of(shape, dtype):
    return jax.ShapeDtypeStruct(shape, dtype)


def params():
    return pltpu.CompilerParams(vmem_limit_bytes=VMEM_LIMIT)


def small(kernel, name, in_specs, out_spec, out_shape):
    return pl.pallas_call(
        kernel, in_specs=in_specs, out_specs=out_spec, out_shape=out_shape, name=name
    )


def cost(keys, matmuls, heads):
    rows = heads * GRP * TOK
    return pl.CostEstimate(
        flops=2 * matmuls * rows * keys * HD * 2,
        bytes_accessed=heads * (2 << 20),
        transcendentals=rows * keys,
    )


def specs(first):
    wide = pl.BlockSpec((1, TOK, GRP * HD), lambda k: (0, 0, first + k))
    narrow = pl.BlockSpec((1, TOK, HD), lambda k: (0, 0, first + k))
    prompt = pl.BlockSpec((PL, HD), lambda k: (0, first + k))
    stats = pl.BlockSpec((1, UNITS, 8, LANES), lambda k: (first + k, 0, 0, 0))
    ds = pl.BlockSpec((1, PL, UNITS * LANES), lambda k: (first + k, 0, 0))
    return wide, narrow, prompt, stats, ds


def resp_stats(queries, grad_out, resp_keys, resp_values):
    wide, narrow, _, stats, _ = specs(0)
    return pl.pallas_call(
        resp_stats_kernel,
        grid=(KVH,),
        in_specs=[wide, wide, narrow, narrow],
        out_specs=stats,
        out_shape=shape_of((KVH, UNITS, 8, LANES), F32),
        compiler_params=params(),
        cost_estimate=cost(192, 2, KVH),
        name="resp_stats",
    )(queries, grad_out, resp_keys, resp_values)


def prompt_part(lengths, queries, grad_out, own_keys, own_values, stats_in):
    wide, _, prompt, stats, ds = specs(0)
    return pl.pallas_call(
        prompt_kernel,
        grid=(KVH,),
        in_specs=[in_smem(), wide, wide, prompt, prompt, stats],
        out_specs=[pl.BlockSpec((2, PL, HD), lambda k: (0, 0, k)), ds, stats],
        out_shape=[
            shape_of((2, PL, KVW), BF16),
            shape_of((KVH, PL, UNITS * LANES), BF16),
            shape_of((KVH, UNITS, 8, LANES), F32),
        ],
        scratch_shapes=[pltpu.VMEM((PL, UNITS * LANES), BF16)],
        compiler_params=params(),
        cost_estimate=cost(256, 4, KVH),
        name="prompt_part",
    )(lengths, queries, grad_out, own_keys, own_values, stats_in)


def resp_part(first, heads, operands, earlier):
    wide, narrow, prompt, stats, ds = specs(first)
    queries, resp_keys = operands[0], operands[2]
    in_specs = [wide, wide, narrow, narrow, prompt, ds, stats]
    aliases = {}
    if earlier:
        aliases = {len(in_specs) + i: i for i in range(3)}
        in_specs = in_specs + [pl.BlockSpec(memory_space=pl.ANY)] * 3
    return pl.pallas_call(
        resp_kernel,
        grid=(heads,),
        in_specs=in_specs,
        out_specs=[wide, narrow, narrow],
        out_shape=[
            shape_of(queries.shape, BF16),
            shape_of(resp_keys.shape, BF16),
            shape_of(resp_keys.shape, BF16),
        ],
        scratch_shapes=[
            pltpu.VMEM((TOK, UNITS * LANES), BF16),
            pltpu.VMEM((TOK, UNITS * LANES), BF16),
        ],
        input_output_aliases=aliases,
        compiler_params=params(),
        cost_estimate=cost(256, 5, heads),
        name="resp_part",
    )(*operands, *earlier)


FIRST_HEADS = 3


def per_device(
    queries,
    resp_keys,
    resp_values,
    grad_out,
    prompt_keys,
    prompt_values,
    group_sizes,
    slot_response,
    lengths,
):
    planes = lax.axis_size("prompt")
    lines = lax.axis_size("resp")
    mates = 2 * lines
    groups = [[g * mates + j for j in range(mates)] for g in range(planes // 2)]
    first = (lax.axis_index("prompt") // 2 * mates).astype(jnp.int32).reshape(1)

    index = small(
        index_kernel,
        "prompt_index",
        [in_smem()] * 3,
        in_smem(),
        shape_of((mates,), jnp.int32),
    )(group_sizes, slot_response, first)
    spread = small(
        spread_kernel,
        "spread",
        [in_vmem()] * 2,
        in_vmem(),
        shape_of((NPROMPT, ROWS, KVW), BF16),
    )(prompt_keys, prompt_values)
    every = lax.all_to_all(spread, "prompt", 0, 0)
    chosen = small(
        select_kernel,
        "select",
        [in_smem(), in_vmem()],
        in_vmem(),
        shape_of((mates, ROWS, KVW), BF16),
    )(index, every)
    queries, chosen = lax.optimization_barrier((queries, chosen))
    own = lax.all_to_all(chosen, BOTH, 0, 0, axis_index_groups=groups)
    stats = resp_stats(queries, grad_out, resp_keys, resp_values)
    own = own.reshape(2, PL, KVW)
    grad_p, ds, final = prompt_part(lengths, queries, grad_out, own[0], own[1], stats)
    terms = lax.all_to_all(
        grad_p.reshape(mates, ROWS, KVW), BOTH, 0, 0, axis_index_groups=groups
    )
    operands = (queries, grad_out, resp_keys, resp_values, own[0], ds, final)
    earlier = resp_part(0, FIRST_HEADS, operands, ())
    terms, *earlier = lax.optimization_barrier((terms, *earlier))
    sums = small(
        sum_kernel,
        "sum_terms",
        [in_smem(), in_vmem()],
        in_vmem(),
        shape_of((NPROMPT, ROWS, KVW), F32),
    )(index, terms)
    sums, *earlier = lax.optimization_barrier((sums, *earlier))
    owned = lax.all_to_all(sums, "prompt", 0, 0)
    grad_q, grad_rk, grad_rv = resp_part(
        FIRST_HEADS, KVH - FIRST_HEADS, operands, tuple(earlier)
    )
    grad_pk, grad_pv = small(
        join_kernel,
        "join",
        [in_vmem()],
        [in_vmem()] * 2,
        [shape_of(prompt_keys.shape, F32), shape_of(prompt_values.shape, F32)],
    )(owned)
    return (grad_q, grad_rk, grad_rv, grad_pk, grad_pv)


def solution(mesh):
    in_specs = (
        P(BOTH, None, None),
        P(BOTH, None, None),
        P(BOTH, None, None),
        P(BOTH, None, None),
        P("prompt", "resp", None),
        P("prompt", "resp", None),
        P(),
        P(),
        P(BOTH),
    )
    out_specs = (
        P(BOTH, None, None),
        P(BOTH, None, None),
        P(BOTH, None, None),
        P("prompt", "resp", None),
        P("prompt", "resp", None),
    )
    return jax.shard_map(
        per_device, mesh=mesh, in_specs=in_specs, out_specs=out_specs, check_vma=False
    )
```

```python
import math

import jax
import jax.numpy as jnp
from jax import lax
from jax.experimental import pallas as pl
from jax.experimental.pallas import tpu as pltpu
from jax.sharding import PartitionSpec as P

KVH = 4
HD = 128
GRP = 8
HEADS = KVH * GRP
DEAD = 1e30
TOK = 256
HALF = 128
PL = 256
ROWS = 16
KVW = KVH * HD
NPROMPT = 8
PAIRS = GRP // 2
UNITS = 2 * PAIRS
LANES = 2 * HALF
SCALING = 1.0 / math.sqrt(HD)
EXP2_SCALE = SCALING * math.log2(math.e)
BF16 = jnp.bfloat16
F32 = jnp.float32
VMEM_LIMIT = 119 * 512 * 1024
SMALL_LIMIT = 4 * 1024 * 1024
PROMPT_LIMIT = 24 * 1024 * 1024
BOTH = ("prompt", "resp")


def contract_last(a, b):
    return lax.dot_general(a, b, (((1,), (1,)), ((), ())), preferred_element_type=F32)


def matmul(a, b):
    return jnp.dot(a, b, preferred_element_type=F32)


def index_kernel(sizes_ref, slots_ref, first_ref, out_ref):
    def body(j, carry):
        slot = slots_ref[first_ref[0] + j]
        found = jnp.int32(0)
        end = jnp.int32(0)
        for p in range(NPROMPT - 1):
            end = end + sizes_ref[p]
            found = found + (slot >= end).astype(jnp.int32)
        out_ref[j] = found
        return carry

    lax.fori_loop(0, out_ref.shape[0], body, 0)


def spread_kernel(keys_hbm, values_hbm, out_ref, sems):
    copies = [
        pltpu.make_async_copy(ref.at[0], out_ref.at[i], sems.at[i])
        for i, ref in enumerate((keys_hbm, values_hbm))
    ]
    for copy in copies:
        copy.start()
    for copy in copies:
        copy.wait()
    for i in range(2, NPROMPT):
        out_ref[i] = out_ref[i % 2]


def select_kernel(index_ref, blocks_ref, out_ref):
    for j in range(out_ref.shape[0]):
        out_ref[j] = blocks_ref[index_ref[j]]


def sum_kernel(index_ref, terms_ref, out_ref, acc_ref):
    acc_ref[...] = jnp.zeros_like(acc_ref)
    for j in range(terms_ref.shape[0]):
        acc_ref[index_ref[j]] += terms_ref[j].astype(F32)
    out_ref[...] = acc_ref[...].astype(BF16)


def join_kernel(blocks_ref, keys_ref, values_ref):
    for first, out_ref in ((0, keys_ref), (1, values_ref)):
        terms = [blocks_ref[i].astype(F32) for i in range(first, NPROMPT, 2)]
        out_ref[0] = (terms[0] + terms[1]) + (terms[2] + terms[3])


def unit_rows(ref, pair, upper):
    rows = slice(upper * HALF, (upper + 1) * HALF)
    at = pair * 2 * HD
    return jnp.concatenate(
        [ref[0, rows, at : at + HD], ref[0, rows, at + HD : at + 2 * HD]], axis=0
    )


def all_rows(ref):
    return jnp.concatenate(
        [unit_rows(ref, pair, upper) for upper in range(2) for pair in range(PAIRS)], axis=0
    )


def resp_scores(kr, q, upper):
    count = HALF * (1 + upper)
    s = contract_last(kr[:count], q)
    lane = lax.broadcasted_iota(jnp.int32, (HALF, LANES), 1) % HALF
    causal = lax.broadcasted_iota(jnp.int32, (HALF, LANES), 0) <= lane
    last = jnp.where(causal, s[count - HALF :], -1e30)
    if upper:
        return jnp.concatenate([s[:HALF], last], axis=0)
    return last


def resp_stats_kernel(q_ref, do_ref, kr_ref, vr_ref, stats_ref):
    kr = kr_ref[0]
    vr = vr_ref[0]
    for upper in range(2):
        for pair in range(PAIRS):
            q = unit_rows(q_ref, pair, upper)
            do = unit_rows(do_ref, pair, upper)
            s = resp_scores(kr, q, upper)
            d = contract_last(vr[: HALF * (1 + upper)], do)
            m = jnp.max(s, axis=0, keepdims=True)
            e = jnp.exp2(s * EXP2_SCALE - m * EXP2_SCALE)
            total = jnp.sum(e, axis=0, keepdims=True)
            weighted = jnp.sum(e * d, axis=0, keepdims=True)
            rows = slice(upper * HALF, (upper + 1) * HALF)
            for i, value in enumerate((m, total, weighted)):
                stats_ref[2 * pair, i : i + 1, rows] = value[:, :HALF]
                stats_ref[2 * pair + 1, i : i + 1, rows] = value[:, HALF:]


def prompt_kernel(
    length_ref, q_ref, do_ref, kp_ref, vp_ref, stats_ref,
    grad_ref, keys_ref, ds_ref, final_ref, p_ref,
):
    length = length_ref[0]
    kp = kp_ref[0]
    vp = vp_ref[0]
    lane = lax.broadcasted_iota(jnp.int32, (1, TOK), 1)
    heads = [slice(h * HD, (h + 1) * HD) for h in range(GRP)]
    for h in range(GRP):
        q = q_ref[0, :, heads[h]]
        do = do_ref[0, :, heads[h]]
        s = contract_last(kp, q)
        d = contract_last(vp, do)
        resp_m = stats_ref[h, 0:1]
        m = jnp.maximum(jnp.max(s, axis=0, keepdims=True), resp_m)
        e = jnp.exp2(s * EXP2_SCALE - m * EXP2_SCALE)
        fade = jnp.exp2((resp_m - m) * EXP2_SCALE)
        total = jnp.sum(e, axis=0, keepdims=True) + fade * stats_ref[h, 1:2]
        weighted = jnp.sum(e * d, axis=0, keepdims=True) + fade * stats_ref[h, 2:3]
        r = weighted / total
        z = jnp.where(lane < length, m * EXP2_SCALE + jnp.log2(total), DEAD)
        p = jnp.exp2(s * EXP2_SCALE - z)
        cols = slice(h * TOK, (h + 1) * TOK)
        ds_ref[:, cols] = (p * (d - r)).astype(BF16)
        p_ref[:, cols] = p.astype(BF16)
        final_ref[h, 0:1] = z
        final_ref[h, 1:2] = r
    dk = matmul(ds_ref[...], jnp.concatenate([q_ref[0, :, c] for c in heads], axis=0))
    dv = matmul(p_ref[...], jnp.concatenate([do_ref[0, :, c] for c in heads], axis=0))
    grad_ref[0] = (dk * SCALING).astype(BF16)
    grad_ref[1] = dv.astype(BF16)
    keys_ref[...] = kp


def resp_kernel(
    q_ref, do_ref, kr_ref, vr_ref, kp_ref, ds_hbm, final_ref,
    dq_ref, dkr_ref, dvr_ref, dsr_ref, p_ref, ds_ref, sems,
):
    step = pl.program_id(0)
    slot = step % 2

    def load(k):
        cols = pl.ds(pl.multiple_of(k * (GRP * TOK), GRP * TOK), GRP * TOK)
        return pltpu.make_async_copy(ds_hbm.at[:, cols], ds_ref.at[k % 2], sems.at[k % 2])

    @pl.when(step == 0)
    def _():
        load(step).start()

    @pl.when(step < KVH - 1)
    def _():
        load(step + 1).start()

    kr = kr_ref[0]
    vr = vr_ref[0]
    keys_t = jnp.transpose(jnp.concatenate([kp_ref[...], kr], axis=0))
    units = [(upper, pair) for upper in range(2) for pair in range(PAIRS)]
    for unit, (upper, pair) in enumerate(units):
        count = HALF * (1 + upper)
        rows = slice(upper * HALF, (upper + 1) * HALF)
        q = unit_rows(q_ref, pair, upper)
        do = unit_rows(do_ref, pair, upper)
        s = resp_scores(kr, q, upper)
        d = contract_last(vr[:count], do)
        z, r = (
            jnp.concatenate(
                [final_ref[h, i : i + 1, rows] for h in (2 * pair, 2 * pair + 1)], axis=1
            )
            for i in range(2)
        )
        p = jnp.exp2(s * EXP2_SCALE - z)
        cols = slice(unit * LANES, (unit + 1) * LANES)
        dsr_ref[:count, cols] = (p * (d - r)).astype(BF16)
        p_ref[:count, cols] = p.astype(BF16)
    load(step).wait()
    for unit, (upper, pair) in enumerate(units):
        count = HALF * (1 + upper)
        rows = slice(upper * HALF, (upper + 1) * HALF)
        cols = slice(unit * LANES, (unit + 1) * LANES)
        prompt_ds = jnp.concatenate(
            [
                ds_ref[slot, :, h * TOK + upper * HALF : h * TOK + (upper + 1) * HALF]
                for h in (2 * pair, 2 * pair + 1)
            ],
            axis=1,
        )
        both = jnp.concatenate([prompt_ds, dsr_ref[:count, cols]], axis=0)
        dq = (jnp.transpose(matmul(keys_t[:, : PL + count], both)) * SCALING).astype(BF16)
        at = pair * 2 * HD
        dq_ref[0, rows, at : at + HD] = dq[:HALF]
        dq_ref[0, rows, at + HD : at + 2 * HD] = dq[HALF:]
    for out_ref, left_ref, right_ref, scale in (
        (dkr_ref, dsr_ref, q_ref, SCALING),
        (dvr_ref, p_ref, do_ref, 1.0),
    ):
        right = all_rows(right_ref)
        split = PAIRS * LANES
        out_ref[0, :HALF] = (matmul(left_ref[:HALF], right) * scale).astype(BF16)
        out_ref[0, HALF:] = (matmul(left_ref[HALF:, split:], right[split:]) * scale).astype(BF16)


def in_smem():
    return pl.BlockSpec(memory_space=pltpu.SMEM)


def in_vmem():
    return pl.BlockSpec(memory_space=pltpu.VMEM)


def shape_of(shape, dtype):
    return jax.ShapeDtypeStruct(shape, dtype)


def params():
    return pltpu.CompilerParams(vmem_limit_bytes=VMEM_LIMIT)


def small(kernel, name, in_specs, out_spec, out_shape, limit=SMALL_LIMIT):
    return pl.pallas_call(
        kernel,
        in_specs=in_specs,
        out_specs=out_spec,
        out_shape=out_shape,
        compiler_params=pltpu.CompilerParams(vmem_limit_bytes=limit),
        name=name,
    )


def cost(keys, matmuls, heads):
    rows = heads * GRP * TOK
    return pl.CostEstimate(
        flops=2 * matmuls * rows * keys * HD * 2,
        bytes_accessed=heads * (2 << 20),
        transcendentals=rows * keys,
    )


def specs(first):
    wide = pl.BlockSpec((1, TOK, GRP * HD), lambda k: (0, 0, first + k))
    narrow = pl.BlockSpec((1, TOK, HD), lambda k: (0, 0, first + k))
    prompt = pl.BlockSpec((PL, HD), lambda k: (0, first + k))
    stats = pl.BlockSpec((GRP, 8, TOK), lambda k: (first + k, 0, 0))
    ds = pl.BlockSpec((PL, GRP * TOK), lambda k: (0, first + k))
    return wide, narrow, prompt, stats, ds


def resp_stats(queries, grad_out, resp_keys, resp_values):
    wide, narrow, _, stats, _ = specs(0)
    return pl.pallas_call(
        resp_stats_kernel,
        grid=(KVH,),
        in_specs=[wide, wide, narrow, narrow],
        out_specs=stats,
        out_shape=shape_of((HEADS, 8, TOK), F32),
        compiler_params=params(),
        cost_estimate=cost(192, 2, KVH),
        name="resp_stats",
    )(queries, grad_out, resp_keys, resp_values)


def prompt_part(lengths, own, queries, grad_out, stats):
    queries, grad_out, stats = (
        pltpu.with_memory_space_constraint(x, pltpu.HBM) for x in (queries, grad_out, stats)
    )
    wide = pl.BlockSpec((1, TOK, GRP * HD), lambda g: (0, 0, g))
    stat = pl.BlockSpec((GRP, 8, TOK), lambda g: (g, 0, 0))
    return pl.pallas_call(
        prompt_kernel,
        grid=(KVH,),
        in_specs=[
            in_smem(),
            wide,
            wide,
            pl.BlockSpec((1, PL, HD), lambda g: (0, 0, g)),
            pl.BlockSpec((1, PL, HD), lambda g: (1, 0, g)),
            stat,
        ],
        out_specs=[
            pl.BlockSpec((2, PL, HD), lambda g: (0, 0, g)),
            pl.BlockSpec((PL, HD), lambda g: (0, g)),
            pl.BlockSpec((PL, GRP * TOK), lambda g: (0, g)),
            stat,
        ],
        out_shape=[
            pltpu.HBM((2, PL, KVW), BF16),
            pltpu.HBM((PL, KVW), BF16),
            pltpu.HBM((PL, HEADS * TOK), BF16),
            pltpu.HBM((HEADS, 8, TOK), F32),
        ],
        scratch_shapes=[
            pltpu.VMEM((PL, GRP * TOK), BF16),
        ],
        compiler_params=pltpu.CompilerParams(vmem_limit_bytes=PROMPT_LIMIT),
        cost_estimate=cost(256, 4, KVH),
        name="prompt_part",
    )(lengths, queries, grad_out, own, own, stats)


def resp_part(queries, grad_out, resp_keys, resp_values, own_keys, ds, final):
    wide, narrow, prompt, stats, _ = specs(0)
    return pl.pallas_call(
        resp_kernel,
        grid=(KVH,),
        in_specs=[
            wide, wide, narrow, narrow, prompt, pl.BlockSpec(memory_space=pl.ANY), stats,
        ],
        out_specs=[wide, narrow, narrow],
        out_shape=[
            shape_of(queries.shape, BF16),
            shape_of(resp_keys.shape, BF16),
            shape_of(resp_keys.shape, BF16),
        ],
        scratch_shapes=[
            pltpu.VMEM((TOK, UNITS * LANES), BF16),
            pltpu.VMEM((TOK, UNITS * LANES), BF16),
            pltpu.VMEM((2, PL, GRP * TOK), BF16),
            pltpu.SemaphoreType.DMA((2,)),
        ],
        compiler_params=params(),
        cost_estimate=cost(256, 5, KVH),
        name="resp_part",
    )(queries, grad_out, resp_keys, resp_values, own_keys, ds, final)


def per_device(
    queries,
    resp_keys,
    resp_values,
    grad_out,
    prompt_keys,
    prompt_values,
    group_sizes,
    slot_response,
    lengths,
):
    planes = lax.axis_size("prompt")
    lines = lax.axis_size("resp")
    mates = 2 * lines
    groups = [[g * mates + j for j in range(mates)] for g in range(planes // 2)]
    first = (lax.axis_index("prompt") // 2 * mates).astype(jnp.int32).reshape(1)

    index = small(
        index_kernel,
        "prompt_index",
        [in_smem()] * 3,
        in_smem(),
        pltpu.SMEM((mates,), jnp.int32),
        VMEM_LIMIT,
    )(group_sizes, slot_response, first)
    spread = pl.pallas_call(
        spread_kernel,
        in_specs=[pl.BlockSpec(memory_space=pl.ANY)] * 2,
        out_specs=in_vmem(),
        out_shape=pltpu.VMEM((NPROMPT, ROWS, KVW), BF16),
        scratch_shapes=[pltpu.SemaphoreType.DMA((2,))],
        compiler_params=params(),
        name="spread",
    )(prompt_keys, prompt_values)
    every = lax.all_to_all(spread, "prompt", 0, 0)
    chosen = small(
        select_kernel,
        "select",
        [in_smem(), in_vmem()],
        in_vmem(),
        shape_of((mates, ROWS, KVW), BF16),
    )(index, every)
    queries, chosen = lax.optimization_barrier((queries, chosen))
    own = lax.all_to_all(chosen, BOTH, 0, 0, axis_index_groups=groups)
    stats = resp_stats(queries, grad_out, resp_keys, resp_values)
    own = own.reshape(2, PL, KVW)
    grad_p, own_keys, ds, final = prompt_part(lengths, own, queries, grad_out, stats)
    terms = lax.all_to_all(
        grad_p.reshape(mates, ROWS, KVW), BOTH, 0, 0, axis_index_groups=groups
    )
    grads = resp_part(queries, grad_out, resp_keys, resp_values, own_keys, ds, final)
    terms, *grads = lax.optimization_barrier((terms, *grads))
    sums = pl.pallas_call(
        sum_kernel,
        in_specs=[in_smem(), in_vmem()],
        out_specs=in_vmem(),
        out_shape=pltpu.VMEM((NPROMPT, ROWS, KVW), BF16),
        scratch_shapes=[pltpu.VMEM((NPROMPT, ROWS, KVW), F32)],
        compiler_params=pltpu.CompilerParams(vmem_limit_bytes=SMALL_LIMIT),
        name="sum_terms",
    )(index, terms)
    owned = lax.all_to_all(sums, "prompt", 0, 0)
    grad_pk, grad_pv = small(
        join_kernel,
        "join",
        [in_vmem()],
        [in_vmem()] * 2,
        [shape_of(prompt_keys.shape, F32), shape_of(prompt_values.shape, F32)],
    )(owned)
    return (*grads, grad_pk, grad_pv)


def solution(mesh):
    in_specs = (
        P(BOTH, None, None),
        P(BOTH, None, None),
        P(BOTH, None, None),
        P(BOTH, None, None),
        P("prompt", "resp", None),
        P("prompt", "resp", None),
        P(),
        P(),
        P(BOTH),
    )
    out_specs = (
        P(BOTH, None, None),
        P(BOTH, None, None),
        P(BOTH, None, None),
        P("prompt", "resp", None),
        P("prompt", "resp", None),
    )
    return jax.shard_map(
        per_device, mesh=mesh, in_specs=in_specs, out_specs=out_specs, check_vma=False
    )
```

```python
import functools
import math

import jax
import jax.numpy as jnp
from jax import lax
from jax.experimental import pallas as pl
from jax.experimental.pallas import tpu as pltpu
from jax.sharding import PartitionSpec as P

KVH = 4
HD = 128
GRP = 8
HEADS = KVH * GRP
DEAD = 1e30
LINES = (14, 4, 0, 5, 7, 8, 1, 3, 6, 9, 11, 12, 2, 10, 13, 15)
FIRST_PLANE = 4
TOK = 256
HALF = 128
PL = 256
ROWS = 16
KVW = KVH * HD
NPROMPT = 8
PAIRS = GRP // 2
UNITS = 2 * PAIRS
LANES = 2 * HALF
SCALING = 1.0 / math.sqrt(HD)
EXP2_SCALE = SCALING * math.log2(math.e)
BF16 = jnp.bfloat16
F32 = jnp.float32
VMEM_LIMIT = 119 * 512 * 1024
SMALL_LIMIT = 4 * 1024 * 1024
PROMPT_LIMIT = 24 * 1024 * 1024
BOTH = ("prompt", "resp")


def contract_last(a, b):
    return lax.dot_general(a, b, (((1,), (1,)), ((), ())), preferred_element_type=F32)


def matmul(a, b):
    return jnp.dot(a, b, preferred_element_type=F32)


def prepare_kernel(
    order, turn,
    keys_hbm, values_hbm, sizes_hbm, slots_hbm, first_ref,
    out_ref, index_ref, sizes_ref, slots_ref, sems,
):
    copies = [
        pltpu.make_async_copy(src, dst, sems.at[i])
        for i, (src, dst) in enumerate(
            (
                (sizes_hbm, sizes_ref),
                (slots_hbm, slots_ref),
                (keys_hbm.at[0], out_ref.at[0]),
                (values_hbm.at[0], out_ref.at[1]),
            )
        )
    ]
    for copy in copies:
        copy.start()
    copies[0].wait()
    copies[1].wait()
    ends = [sizes_ref[0]]
    for p in range(1, NPROMPT - 1):
        ends.append(ends[-1] + sizes_ref[p])
    for j, member in enumerate(order):
        slot = slots_ref[first_ref[0] + member]
        found = jnp.int32(0)
        for end in ends:
            found = found + (slot >= end).astype(jnp.int32)
        found = found + (NPROMPT - turn)
        index_ref[j] = jnp.where(found >= NPROMPT, found - NPROMPT, found)
    copies[2].wait()
    copies[3].wait()
    for i in range(2, NPROMPT):
        out_ref[i] = out_ref[i % 2]


def select_kernel(index_ref, blocks_ref, out_ref):
    for j in range(out_ref.shape[0]):
        out_ref[j] = blocks_ref[index_ref[j]]


def sum_kernel(index_ref, terms_ref, out_ref, acc_ref):
    acc_ref[...] = jnp.zeros_like(acc_ref)
    for j in range(terms_ref.shape[0]):
        acc_ref[index_ref[j]] += terms_ref[j].astype(F32)
    out_ref[...] = acc_ref[...].astype(BF16)


def join_kernel(blocks_ref, keys_ref, values_ref):
    for first, out_ref in ((0, keys_ref), (1, values_ref)):
        terms = [blocks_ref[i].astype(F32) for i in range(first, NPROMPT, 2)]
        out_ref[0] = (terms[0] + terms[1]) + (terms[2] + terms[3])


def unit_rows(ref, pair, upper):
    rows = slice(upper * HALF, (upper + 1) * HALF)
    at = pair * 2 * HD
    return jnp.concatenate(
        [ref[0, rows, at : at + HD], ref[0, rows, at + HD : at + 2 * HD]], axis=0
    )


def all_rows(ref):
    return jnp.concatenate(
        [unit_rows(ref, pair, upper) for upper in range(2) for pair in range(PAIRS)], axis=0
    )


def resp_scores(kr, q, upper):
    count = HALF * (1 + upper)
    s = contract_last(kr[:count], q)
    lane = lax.broadcasted_iota(jnp.int32, (HALF, LANES), 1) % HALF
    causal = lax.broadcasted_iota(jnp.int32, (HALF, LANES), 0) <= lane
    last = jnp.where(causal, s[count - HALF :], -1e30)
    if upper:
        return jnp.concatenate([s[:HALF], last], axis=0)
    return last


def resp_stats_kernel(q_ref, do_ref, kr_ref, vr_ref, stats_ref):
    kr = kr_ref[0]
    vr = vr_ref[0]
    for upper in range(2):
        for pair in range(PAIRS):
            q = unit_rows(q_ref, pair, upper)
            do = unit_rows(do_ref, pair, upper)
            s = resp_scores(kr, q, upper)
            d = contract_last(vr[: HALF * (1 + upper)], do)
            m = jnp.max(s, axis=0, keepdims=True)
            e = jnp.exp2(s * EXP2_SCALE - m * EXP2_SCALE)
            total = jnp.sum(e, axis=0, keepdims=True)
            weighted = jnp.sum(e * d, axis=0, keepdims=True)
            rows = slice(upper * HALF, (upper + 1) * HALF)
            for i, value in enumerate((m, total, weighted)):
                stats_ref[2 * pair, i : i + 1, rows] = value[:, :HALF]
                stats_ref[2 * pair + 1, i : i + 1, rows] = value[:, HALF:]


def prompt_kernel(
    length_ref, q_ref, do_ref, kp_ref, vp_ref, stats_ref,
    grad_ref, keys_ref, ds_ref, final_ref, p_ref,
):
    length = length_ref[0]
    kp = kp_ref[0]
    vp = vp_ref[0]
    lane = lax.broadcasted_iota(jnp.int32, (1, TOK), 1)
    heads = [slice(h * HD, (h + 1) * HD) for h in range(GRP)]
    for h in range(GRP):
        q = q_ref[0, :, heads[h]]
        do = do_ref[0, :, heads[h]]
        s = contract_last(kp, q)
        d = contract_last(vp, do)
        resp_m = stats_ref[h, 0:1]
        m = jnp.maximum(jnp.max(s, axis=0, keepdims=True), resp_m)
        e = jnp.exp2(s * EXP2_SCALE - m * EXP2_SCALE)
        fade = jnp.exp2((resp_m - m) * EXP2_SCALE)
        total = jnp.sum(e, axis=0, keepdims=True) + fade * stats_ref[h, 1:2]
        weighted = jnp.sum(e * d, axis=0, keepdims=True) + fade * stats_ref[h, 2:3]
        r = weighted / total
        z = jnp.where(lane < length, m * EXP2_SCALE + jnp.log2(total), DEAD)
        p = jnp.exp2(s * EXP2_SCALE - z)
        cols = slice(h * TOK, (h + 1) * TOK)
        ds_ref[:, cols] = (p * (d - r)).astype(BF16)
        p_ref[:, cols] = p.astype(BF16)
        final_ref[h, 0:1] = z
        final_ref[h, 1:2] = r
    dk = matmul(ds_ref[...], jnp.concatenate([q_ref[0, :, c] for c in heads], axis=0))
    dv = matmul(p_ref[...], jnp.concatenate([do_ref[0, :, c] for c in heads], axis=0))
    grad_ref[0] = (dk * SCALING).astype(BF16)
    grad_ref[1] = dv.astype(BF16)
    keys_ref[...] = kp


def resp_kernel(
    q_ref, do_ref, kr_ref, vr_ref, kp_ref, ds_hbm, final_ref,
    dq_ref, dkr_ref, dvr_ref, dsr_ref, p_ref, ds_ref, sems,
):
    step = pl.program_id(0)
    slot = step % 2

    def load(k):
        cols = pl.ds(pl.multiple_of(k * (GRP * TOK), GRP * TOK), GRP * TOK)
        return pltpu.make_async_copy(ds_hbm.at[:, cols], ds_ref.at[k % 2], sems.at[k % 2])

    @pl.when(step == 0)
    def _():
        load(step).start()

    @pl.when(step < KVH - 1)
    def _():
        load(step + 1).start()

    kr = kr_ref[0]
    vr = vr_ref[0]
    keys_t = jnp.transpose(jnp.concatenate([kp_ref[...], kr], axis=0))
    units = [(upper, pair) for upper in range(2) for pair in range(PAIRS)]
    for unit, (upper, pair) in enumerate(units):
        count = HALF * (1 + upper)
        rows = slice(upper * HALF, (upper + 1) * HALF)
        q = unit_rows(q_ref, pair, upper)
        do = unit_rows(do_ref, pair, upper)
        s = resp_scores(kr, q, upper)
        d = contract_last(vr[:count], do)
        z, r = (
            jnp.concatenate(
                [final_ref[h, i : i + 1, rows] for h in (2 * pair, 2 * pair + 1)], axis=1
            )
            for i in range(2)
        )
        p = jnp.exp2(s * EXP2_SCALE - z)
        cols = slice(unit * LANES, (unit + 1) * LANES)
        dsr_ref[:count, cols] = (p * (d - r)).astype(BF16)
        p_ref[:count, cols] = p.astype(BF16)
    load(step).wait()
    for unit, (upper, pair) in enumerate(units):
        count = HALF * (1 + upper)
        rows = slice(upper * HALF, (upper + 1) * HALF)
        cols = slice(unit * LANES, (unit + 1) * LANES)
        prompt_ds = jnp.concatenate(
            [
                ds_ref[slot, :, h * TOK + upper * HALF : h * TOK + (upper + 1) * HALF]
                for h in (2 * pair, 2 * pair + 1)
            ],
            axis=1,
        )
        both = jnp.concatenate([prompt_ds, dsr_ref[:count, cols]], axis=0)
        dq = (jnp.transpose(matmul(keys_t[:, : PL + count], both)) * SCALING).astype(BF16)
        at = pair * 2 * HD
        dq_ref[0, rows, at : at + HD] = dq[:HALF]
        dq_ref[0, rows, at + HD : at + 2 * HD] = dq[HALF:]
    for out_ref, left_ref, right_ref, scale in (
        (dkr_ref, dsr_ref, q_ref, SCALING),
        (dvr_ref, p_ref, do_ref, 1.0),
    ):
        right = all_rows(right_ref)
        split = PAIRS * LANES
        out_ref[0, :HALF] = (matmul(left_ref[:HALF], right) * scale).astype(BF16)
        out_ref[0, HALF:] = (matmul(left_ref[HALF:, split:], right[split:]) * scale).astype(BF16)


def in_smem():
    return pl.BlockSpec(memory_space=pltpu.SMEM)


def in_vmem():
    return pl.BlockSpec(memory_space=pltpu.VMEM)


def shape_of(shape, dtype):
    return jax.ShapeDtypeStruct(shape, dtype)


def params():
    return pltpu.CompilerParams(vmem_limit_bytes=VMEM_LIMIT)


def small(kernel, name, in_specs, out_spec, out_shape, limit=SMALL_LIMIT):
    return pl.pallas_call(
        kernel,
        in_specs=in_specs,
        out_specs=out_spec,
        out_shape=out_shape,
        compiler_params=pltpu.CompilerParams(vmem_limit_bytes=limit),
        name=name,
    )


def cost(keys, matmuls, heads):
    rows = heads * GRP * TOK
    return pl.CostEstimate(
        flops=2 * matmuls * rows * keys * HD * 2,
        bytes_accessed=heads * (2 << 20),
        transcendentals=rows * keys,
    )


def specs(first):
    wide = pl.BlockSpec((1, TOK, GRP * HD), lambda k: (0, 0, first + k))
    narrow = pl.BlockSpec((1, TOK, HD), lambda k: (0, 0, first + k))
    prompt = pl.BlockSpec((PL, HD), lambda k: (0, first + k))
    stats = pl.BlockSpec((GRP, 8, TOK), lambda k: (first + k, 0, 0))
    ds = pl.BlockSpec((PL, GRP * TOK), lambda k: (0, first + k))
    return wide, narrow, prompt, stats, ds


def resp_stats(queries, grad_out, resp_keys, resp_values):
    wide, narrow, _, stats, _ = specs(0)
    return pl.pallas_call(
        resp_stats_kernel,
        grid=(KVH,),
        in_specs=[wide, wide, narrow, narrow],
        out_specs=stats,
        out_shape=shape_of((HEADS, 8, TOK), F32),
        compiler_params=params(),
        cost_estimate=cost(192, 2, KVH),
        name="resp_stats",
    )(queries, grad_out, resp_keys, resp_values)


def prompt_part(lengths, own, queries, grad_out, stats):
    queries, grad_out, stats = (
        pltpu.with_memory_space_constraint(x, pltpu.HBM) for x in (queries, grad_out, stats)
    )
    wide = pl.BlockSpec((1, TOK, GRP * HD), lambda g: (0, 0, g))
    stat = pl.BlockSpec((GRP, 8, TOK), lambda g: (g, 0, 0))
    return pl.pallas_call(
        prompt_kernel,
        grid=(KVH,),
        in_specs=[
            in_smem(),
            wide,
            wide,
            pl.BlockSpec((1, PL, HD), lambda g: (0, 0, g)),
            pl.BlockSpec((1, PL, HD), lambda g: (1, 0, g)),
            stat,
        ],
        out_specs=[
            pl.BlockSpec((2, PL, HD), lambda g: (0, 0, g)),
            pl.BlockSpec((PL, HD), lambda g: (0, g)),
            pl.BlockSpec((PL, GRP * TOK), lambda g: (0, g)),
            stat,
        ],
        out_shape=[
            pltpu.HBM((2, PL, KVW), BF16),
            pltpu.HBM((PL, KVW), BF16),
            pltpu.HBM((PL, HEADS * TOK), BF16),
            pltpu.HBM((HEADS, 8, TOK), F32),
        ],
        scratch_shapes=[
            pltpu.VMEM((PL, GRP * TOK), BF16),
        ],
        compiler_params=pltpu.CompilerParams(vmem_limit_bytes=PROMPT_LIMIT),
        cost_estimate=cost(256, 4, KVH),
        name="prompt_part",
    )(lengths, queries, grad_out, own, own, stats)


def resp_part(queries, grad_out, resp_keys, resp_values, own_keys, ds, final):
    wide, narrow, prompt, stats, _ = specs(0)
    return pl.pallas_call(
        resp_kernel,
        grid=(KVH,),
        in_specs=[
            wide, wide, narrow, narrow, prompt, pl.BlockSpec(memory_space=pl.ANY), stats,
        ],
        out_specs=[wide, narrow, narrow],
        out_shape=[
            shape_of(queries.shape, BF16),
            shape_of(resp_keys.shape, BF16),
            shape_of(resp_keys.shape, BF16),
        ],
        scratch_shapes=[
            pltpu.VMEM((TOK, UNITS * LANES), BF16),
            pltpu.VMEM((TOK, UNITS * LANES), BF16),
            pltpu.VMEM((2, PL, GRP * TOK), BF16),
            pltpu.SemaphoreType.DMA((2,)),
        ],
        compiler_params=params(),
        cost_estimate=cost(256, 5, KVH),
        name="resp_part",
    )(queries, grad_out, resp_keys, resp_values, own_keys, ds, final)


def per_device(
    queries,
    resp_keys,
    resp_values,
    grad_out,
    prompt_keys,
    prompt_values,
    group_sizes,
    slot_response,
    lengths,
):
    planes = lax.axis_size("prompt")
    lines = lax.axis_size("resp")
    mates = 2 * lines
    slots = slot_response.shape[0]
    order = [c * lines + b for c in range(2) for b in LINES]
    groups = [[g * mates + j for j in order] for g in range(planes // 2)]
    turn = FIRST_PLANE
    column = [[(i + turn) % planes for i in range(planes)]]
    first = (lax.axis_index("prompt") // 2 * mates).astype(jnp.int32).reshape(1)

    spread, index = pl.pallas_call(
        functools.partial(prepare_kernel, order, turn),
        in_specs=[pl.BlockSpec(memory_space=pl.ANY)] * 4 + [in_smem()],
        out_specs=[in_vmem(), in_smem()],
        out_shape=[
            pltpu.VMEM((NPROMPT, ROWS, KVW), BF16),
            pltpu.SMEM((mates,), jnp.int32),
        ],
        scratch_shapes=[
            pltpu.SMEM((NPROMPT,), jnp.int32),
            pltpu.SMEM((slots,), jnp.int32),
            pltpu.SemaphoreType.DMA((4,)),
        ],
        compiler_params=pltpu.CompilerParams(vmem_limit_bytes=SMALL_LIMIT),
        name="prepare",
    )(
        *(
            pltpu.with_memory_space_constraint(x, pltpu.HBM)
            for x in (prompt_keys, prompt_values, group_sizes, slot_response)
        ),
        first,
    )
    every = lax.all_to_all(spread, "prompt", 0, 0, axis_index_groups=column)
    chosen = small(
        select_kernel,
        "select",
        [in_smem(), in_vmem()],
        in_vmem(),
        shape_of((mates, ROWS, KVW), BF16),
    )(index, every)
    queries, chosen = lax.optimization_barrier((queries, chosen))
    own = lax.all_to_all(chosen, BOTH, 0, 0, axis_index_groups=groups)
    stats = resp_stats(queries, grad_out, resp_keys, resp_values)
    own = own.reshape(2, PL, KVW)
    grad_p, own_keys, ds, final = prompt_part(lengths, own, queries, grad_out, stats)
    terms = lax.all_to_all(
        grad_p.reshape(mates, ROWS, KVW), BOTH, 0, 0, axis_index_groups=groups
    )
    grads = resp_part(queries, grad_out, resp_keys, resp_values, own_keys, ds, final)
    terms, *grads = lax.optimization_barrier((terms, *grads))
    sums = pl.pallas_call(
        sum_kernel,
        in_specs=[in_smem(), in_vmem()],
        out_specs=in_vmem(),
        out_shape=pltpu.VMEM((NPROMPT, ROWS, KVW), BF16),
        scratch_shapes=[pltpu.VMEM((NPROMPT, ROWS, KVW), F32)],
        compiler_params=pltpu.CompilerParams(vmem_limit_bytes=SMALL_LIMIT),
        name="sum_terms",
    )(index, terms)
    owned = lax.all_to_all(sums, "prompt", 0, 0, axis_index_groups=column)
    grad_pk, grad_pv = small(
        join_kernel,
        "join",
        [in_vmem()],
        [in_vmem()] * 2,
        [shape_of(prompt_keys.shape, F32), shape_of(prompt_values.shape, F32)],
    )(owned)
    return (*grads, grad_pk, grad_pv)


def solution(mesh):
    in_specs = (
        P(BOTH, None, None),
        P(BOTH, None, None),
        P(BOTH, None, None),
        P(BOTH, None, None),
        P("prompt", "resp", None),
        P("prompt", "resp", None),
        P(),
        P(),
        P(BOTH),
    )
    out_specs = (
        P(BOTH, None, None),
        P(BOTH, None, None),
        P(BOTH, None, None),
        P("prompt", "resp", None),
        P("prompt", "resp", None),
    )
    return jax.shard_map(
        per_device, mesh=mesh, in_specs=in_specs, out_specs=out_specs, check_vma=False
    )
```

```python
import functools
import math

import jax
import jax.numpy as jnp
from jax import lax
from jax.experimental import pallas as pl
from jax.experimental.pallas import tpu as pltpu
from jax.sharding import PartitionSpec as P

KVH = 4
HD = 128
GRP = 8
HEADS = KVH * GRP
DEAD = 1e30
LINES = (14, 4, 0, 5, 7, 8, 1, 3, 6, 9, 11, 12, 2, 10, 13, 15)
FIRST_PLANE = 4
TOK = 256
HALF = 128
PL = 256
ROWS = 16
KVW = KVH * HD
NPROMPT = 8
PAIRS = GRP // 2
UNITS = 2 * PAIRS
LANES = 2 * HALF
SCALING = 1.0 / math.sqrt(HD)
EXP2_SCALE = SCALING * math.log2(math.e)
BF16 = jnp.bfloat16
F32 = jnp.float32
VMEM_LIMIT = 119 * 512 * 1024
SMALL_LIMIT = 4 * 1024 * 1024
PROMPT_LIMIT = 24 * 1024 * 1024
BOTH = ("prompt", "resp")


def contract_last(a, b):
    return lax.dot_general(a, b, (((1,), (1,)), ((), ())), preferred_element_type=F32)


def matmul(a, b):
    return jnp.dot(a, b, preferred_element_type=F32)


def prepare_kernel(
    order, turn,
    keys_hbm, values_hbm, sizes_hbm, slots_hbm, first_ref,
    out_ref, index_ref, sizes_ref, slots_ref, sems,
):
    copies = [
        pltpu.make_async_copy(src, dst, sems.at[i])
        for i, (src, dst) in enumerate(
            (
                (sizes_hbm, sizes_ref),
                (slots_hbm, slots_ref),
                (keys_hbm.at[0], out_ref.at[1]),
                (values_hbm.at[0], out_ref.at[0]),
            )
        )
    ]
    for copy in copies:
        copy.start()
    copies[0].wait()
    copies[1].wait()
    ends = [sizes_ref[0]]
    for p in range(1, NPROMPT - 1):
        ends.append(ends[-1] + sizes_ref[p])
    for j, member in enumerate(order):
        slot = slots_ref[first_ref[0] + member]
        found = jnp.int32(0)
        for end in ends:
            found = found + (slot >= end).astype(jnp.int32)
        found = found + (NPROMPT - turn)
        found = jnp.where(found >= NPROMPT, found - NPROMPT, found)
        index_ref[j] = found + 1 - 2 * (found & 1)
    copies[2].wait()
    copies[3].wait()
    for i in range(2, NPROMPT):
        out_ref[i] = out_ref[i % 2]


def select_kernel(index_ref, blocks_ref, out_ref):
    for j in range(out_ref.shape[0]):
        out_ref[j] = blocks_ref[index_ref[j]]


def sum_kernel(index_ref, terms_ref, out_ref, acc_ref):
    acc_ref[...] = jnp.zeros_like(acc_ref)
    for j in range(terms_ref.shape[0]):
        acc_ref[index_ref[j]] += terms_ref[j].astype(F32)
    out_ref[...] = acc_ref[...].astype(BF16)


def join_kernel(blocks_ref, keys_ref, values_ref):
    for first, out_ref in ((1, keys_ref), (0, values_ref)):
        terms = [blocks_ref[i].astype(F32) for i in range(first, NPROMPT, 2)]
        out_ref[0] = (terms[0] + terms[1]) + (terms[2] + terms[3])


def unit_rows(ref, pair, upper):
    rows = slice(upper * HALF, (upper + 1) * HALF)
    at = pair * 2 * HD
    return jnp.concatenate(
        [ref[0, rows, at : at + HD], ref[0, rows, at + HD : at + 2 * HD]], axis=0
    )


def all_rows(ref):
    return jnp.concatenate(
        [unit_rows(ref, pair, upper) for upper in range(2) for pair in range(PAIRS)], axis=0
    )


def resp_scores(kr, q, upper):
    count = HALF * (1 + upper)
    s = contract_last(kr[:count], q)
    lane = lax.broadcasted_iota(jnp.int32, (HALF, LANES), 1) % HALF
    causal = lax.broadcasted_iota(jnp.int32, (HALF, LANES), 0) <= lane
    last = jnp.where(causal, s[count - HALF :], -1e30)
    if upper:
        return jnp.concatenate([s[:HALF], last], axis=0)
    return last


def resp_stats_kernel(q_ref, do_ref, kr_ref, vr_ref, stats_ref):
    kr = kr_ref[0]
    vr = vr_ref[0]
    for upper in range(2):
        for pair in range(PAIRS):
            q = unit_rows(q_ref, pair, upper)
            do = unit_rows(do_ref, pair, upper)
            s = resp_scores(kr, q, upper)
            d = contract_last(vr[: HALF * (1 + upper)], do)
            m = jnp.max(s, axis=0, keepdims=True)
            e = jnp.exp2(s * EXP2_SCALE - m * EXP2_SCALE)
            total = jnp.sum(e, axis=0, keepdims=True)
            weighted = jnp.sum(e * d, axis=0, keepdims=True)
            rows = slice(upper * HALF, (upper + 1) * HALF)
            for i, value in enumerate((m, total, weighted)):
                stats_ref[2 * pair, i : i + 1, rows] = value[:, :HALF]
                stats_ref[2 * pair + 1, i : i + 1, rows] = value[:, HALF:]


def prompt_kernel(
    length_ref, q_ref, do_ref, kp_ref, vp_ref, stats_ref,
    grad_ref, keys_ref, ds_ref, final_ref, p_ref,
):
    length = length_ref[0]
    kp = kp_ref[0]
    vp = vp_ref[0]
    lane = lax.broadcasted_iota(jnp.int32, (1, TOK), 1)
    heads = [slice(h * HD, (h + 1) * HD) for h in range(GRP)]
    for h in range(GRP):
        q = q_ref[0, :, heads[h]]
        do = do_ref[0, :, heads[h]]
        s = contract_last(kp, q)
        d = contract_last(vp, do)
        resp_m = stats_ref[h, 0:1]
        m = jnp.maximum(jnp.max(s, axis=0, keepdims=True), resp_m)
        e = jnp.exp2(s * EXP2_SCALE - m * EXP2_SCALE)
        fade = jnp.exp2((resp_m - m) * EXP2_SCALE)
        total = jnp.sum(e, axis=0, keepdims=True) + fade * stats_ref[h, 1:2]
        weighted = jnp.sum(e * d, axis=0, keepdims=True) + fade * stats_ref[h, 2:3]
        r = weighted / total
        z = jnp.where(lane < length, m * EXP2_SCALE + jnp.log2(total), DEAD)
        p = jnp.exp2(s * EXP2_SCALE - z)
        cols = slice(h * TOK, (h + 1) * TOK)
        ds_ref[:, cols] = (p * (d - r)).astype(BF16)
        p_ref[:, cols] = p.astype(BF16)
        final_ref[h, 0:1] = z
        final_ref[h, 1:2] = r
    dk = matmul(ds_ref[...], jnp.concatenate([q_ref[0, :, c] for c in heads], axis=0))
    dv = matmul(p_ref[...], jnp.concatenate([do_ref[0, :, c] for c in heads], axis=0))
    grad_ref[0] = dv.astype(BF16)
    grad_ref[1] = (dk * SCALING).astype(BF16)
    keys_ref[...] = kp


def resp_kernel(
    q_ref, do_ref, kr_ref, vr_ref, kp_ref, ds_hbm, final_ref,
    dq_ref, dkr_ref, dvr_ref, dsr_ref, p_ref, ds_ref, sems,
):
    step = pl.program_id(0)
    slot = step % 2

    def load(k):
        cols = pl.ds(pl.multiple_of(k * (GRP * TOK), GRP * TOK), GRP * TOK)
        return pltpu.make_async_copy(ds_hbm.at[:, cols], ds_ref.at[k % 2], sems.at[k % 2])

    @pl.when(step == 0)
    def _():
        load(step).start()

    @pl.when(step < KVH - 1)
    def _():
        load(step + 1).start()

    kr = kr_ref[0]
    vr = vr_ref[0]
    keys_t = jnp.transpose(jnp.concatenate([kp_ref[...], kr], axis=0))
    units = [(upper, pair) for upper in range(2) for pair in range(PAIRS)]
    for unit, (upper, pair) in enumerate(units):
        count = HALF * (1 + upper)
        rows = slice(upper * HALF, (upper + 1) * HALF)
        q = unit_rows(q_ref, pair, upper)
        do = unit_rows(do_ref, pair, upper)
        s = resp_scores(kr, q, upper)
        d = contract_last(vr[:count], do)
        z, r = (
            jnp.concatenate(
                [final_ref[h, i : i + 1, rows] for h in (2 * pair, 2 * pair + 1)], axis=1
            )
            for i in range(2)
        )
        p = jnp.exp2(s * EXP2_SCALE - z)
        cols = slice(unit * LANES, (unit + 1) * LANES)
        dsr_ref[:count, cols] = (p * (d - r)).astype(BF16)
        p_ref[:count, cols] = p.astype(BF16)
    load(step).wait()
    for unit, (upper, pair) in enumerate(units):
        count = HALF * (1 + upper)
        rows = slice(upper * HALF, (upper + 1) * HALF)
        cols = slice(unit * LANES, (unit + 1) * LANES)
        prompt_ds = jnp.concatenate(
            [
                ds_ref[slot, :, h * TOK + upper * HALF : h * TOK + (upper + 1) * HALF]
                for h in (2 * pair, 2 * pair + 1)
            ],
            axis=1,
        )
        both = jnp.concatenate([prompt_ds, dsr_ref[:count, cols]], axis=0)
        dq = (jnp.transpose(matmul(keys_t[:, : PL + count], both)) * SCALING).astype(BF16)
        at = pair * 2 * HD
        dq_ref[0, rows, at : at + HD] = dq[:HALF]
        dq_ref[0, rows, at + HD : at + 2 * HD] = dq[HALF:]
    for out_ref, left_ref, right_ref, scale in (
        (dkr_ref, dsr_ref, q_ref, SCALING),
        (dvr_ref, p_ref, do_ref, 1.0),
    ):
        right = all_rows(right_ref)
        split = PAIRS * LANES
        out_ref[0, :HALF] = (matmul(left_ref[:HALF], right) * scale).astype(BF16)
        out_ref[0, HALF:] = (matmul(left_ref[HALF:, split:], right[split:]) * scale).astype(BF16)


def in_smem():
    return pl.BlockSpec(memory_space=pltpu.SMEM)


def in_vmem():
    return pl.BlockSpec(memory_space=pltpu.VMEM)


def shape_of(shape, dtype):
    return jax.ShapeDtypeStruct(shape, dtype)


def params():
    return pltpu.CompilerParams(vmem_limit_bytes=VMEM_LIMIT)


def small(kernel, name, in_specs, out_spec, out_shape, limit=SMALL_LIMIT):
    return pl.pallas_call(
        kernel,
        in_specs=in_specs,
        out_specs=out_spec,
        out_shape=out_shape,
        compiler_params=pltpu.CompilerParams(vmem_limit_bytes=limit),
        name=name,
    )


def cost(keys, matmuls, heads):
    rows = heads * GRP * TOK
    return pl.CostEstimate(
        flops=2 * matmuls * rows * keys * HD * 2,
        bytes_accessed=heads * (2 << 20),
        transcendentals=rows * keys,
    )


def specs(first):
    wide = pl.BlockSpec((1, TOK, GRP * HD), lambda k: (0, 0, first + k))
    narrow = pl.BlockSpec((1, TOK, HD), lambda k: (0, 0, first + k))
    prompt = pl.BlockSpec((PL, HD), lambda k: (0, first + k))
    stats = pl.BlockSpec((GRP, 8, TOK), lambda k: (first + k, 0, 0))
    ds = pl.BlockSpec((PL, GRP * TOK), lambda k: (0, first + k))
    return wide, narrow, prompt, stats, ds


def resp_stats(queries, grad_out, resp_keys, resp_values):
    wide, narrow, _, stats, _ = specs(0)
    return pl.pallas_call(
        resp_stats_kernel,
        grid=(KVH,),
        in_specs=[wide, wide, narrow, narrow],
        out_specs=stats,
        out_shape=shape_of((HEADS, 8, TOK), F32),
        compiler_params=params(),
        cost_estimate=cost(192, 2, KVH),
        name="resp_stats",
    )(queries, grad_out, resp_keys, resp_values)


def prompt_part(lengths, own, queries, grad_out, stats):
    queries, grad_out, stats = (
        pltpu.with_memory_space_constraint(x, pltpu.HBM) for x in (queries, grad_out, stats)
    )
    wide = pl.BlockSpec((1, TOK, GRP * HD), lambda g: (0, 0, g))
    stat = pl.BlockSpec((GRP, 8, TOK), lambda g: (g, 0, 0))
    return pl.pallas_call(
        prompt_kernel,
        grid=(KVH,),
        in_specs=[
            in_smem(),
            wide,
            wide,
            pl.BlockSpec((1, PL, HD), lambda g: (1, 0, g)),
            pl.BlockSpec((1, PL, HD), lambda g: (0, 0, g)),
            stat,
        ],
        out_specs=[
            pl.BlockSpec((2, PL, HD), lambda g: (0, 0, g)),
            pl.BlockSpec((PL, HD), lambda g: (0, g)),
            pl.BlockSpec((PL, GRP * TOK), lambda g: (0, g)),
            stat,
        ],
        out_shape=[
            pltpu.HBM((2, PL, KVW), BF16),
            pltpu.HBM((PL, KVW), BF16),
            pltpu.HBM((PL, HEADS * TOK), BF16),
            pltpu.HBM((HEADS, 8, TOK), F32),
        ],
        scratch_shapes=[
            pltpu.VMEM((PL, GRP * TOK), BF16),
        ],
        compiler_params=pltpu.CompilerParams(vmem_limit_bytes=PROMPT_LIMIT),
        cost_estimate=cost(256, 4, KVH),
        name="prompt_part",
    )(lengths, queries, grad_out, own, own, stats)


def resp_part(queries, grad_out, resp_keys, resp_values, own_keys, ds, final):
    wide, narrow, prompt, stats, _ = specs(0)
    return pl.pallas_call(
        resp_kernel,
        grid=(KVH,),
        in_specs=[
            wide, wide, narrow, narrow, prompt, pl.BlockSpec(memory_space=pl.ANY), stats,
        ],
        out_specs=[wide, narrow, narrow],
        out_shape=[
            shape_of(queries.shape, BF16),
            shape_of(resp_keys.shape, BF16),
            shape_of(resp_keys.shape, BF16),
        ],
        scratch_shapes=[
            pltpu.VMEM((TOK, UNITS * LANES), BF16),
            pltpu.VMEM((TOK, UNITS * LANES), BF16),
            pltpu.VMEM((2, PL, GRP * TOK), BF16),
            pltpu.SemaphoreType.DMA((2,)),
        ],
        compiler_params=params(),
        cost_estimate=cost(256, 5, KVH),
        name="resp_part",
    )(queries, grad_out, resp_keys, resp_values, own_keys, ds, final)


def per_device(
    queries,
    resp_keys,
    resp_values,
    grad_out,
    prompt_keys,
    prompt_values,
    group_sizes,
    slot_response,
    lengths,
):
    planes = lax.axis_size("prompt")
    lines = lax.axis_size("resp")
    mates = 2 * lines
    slots = slot_response.shape[0]
    order = [c * lines + b for c in (1, 0) for b in LINES]
    groups = [[g * mates + j for j in order] for g in range(planes // 2)]
    turn = FIRST_PLANE
    column = [[(i + turn) % planes ^ 1 for i in range(planes)]]
    first = (lax.axis_index("prompt") // 2 * mates).astype(jnp.int32).reshape(1)

    spread, index = pl.pallas_call(
        functools.partial(prepare_kernel, order, turn),
        in_specs=[pl.BlockSpec(memory_space=pl.ANY)] * 4 + [in_smem()],
        out_specs=[in_vmem(), in_smem()],
        out_shape=[
            pltpu.VMEM((NPROMPT, ROWS, KVW), BF16),
            pltpu.SMEM((mates,), jnp.int32),
        ],
        scratch_shapes=[
            pltpu.SMEM((NPROMPT,), jnp.int32),
            pltpu.SMEM((slots,), jnp.int32),
            pltpu.SemaphoreType.DMA((4,)),
        ],
        compiler_params=pltpu.CompilerParams(vmem_limit_bytes=SMALL_LIMIT),
        name="prepare",
    )(
        *(
            pltpu.with_memory_space_constraint(x, pltpu.HBM)
            for x in (prompt_keys, prompt_values, group_sizes, slot_response)
        ),
        first,
    )
    every = lax.all_to_all(spread, "prompt", 0, 0, axis_index_groups=column)
    chosen = small(
        select_kernel,
        "select",
        [in_smem(), in_vmem()],
        in_vmem(),
        shape_of((mates, ROWS, KVW), BF16),
    )(index, every)
    queries, chosen = lax.optimization_barrier((queries, chosen))
    own = lax.all_to_all(chosen, BOTH, 0, 0, axis_index_groups=groups)
    stats = resp_stats(queries, grad_out, resp_keys, resp_values)
    own = own.reshape(2, PL, KVW)
    grad_p, own_keys, ds, final = prompt_part(lengths, own, queries, grad_out, stats)
    terms = lax.all_to_all(
        grad_p.reshape(mates, ROWS, KVW), BOTH, 0, 0, axis_index_groups=groups
    )
    grads = resp_part(queries, grad_out, resp_keys, resp_values, own_keys, ds, final)
    terms, *grads = lax.optimization_barrier((terms, *grads))
    sums = pl.pallas_call(
        sum_kernel,
        in_specs=[in_smem(), in_vmem()],
        out_specs=in_vmem(),
        out_shape=pltpu.VMEM((NPROMPT, ROWS, KVW), BF16),
        scratch_shapes=[pltpu.VMEM((NPROMPT, ROWS, KVW), F32)],
        compiler_params=pltpu.CompilerParams(vmem_limit_bytes=SMALL_LIMIT),
        name="sum_terms",
    )(index, terms)
    owned = lax.all_to_all(sums, "prompt", 0, 0, axis_index_groups=column)
    grad_pk, grad_pv = small(
        join_kernel,
        "join",
        [in_vmem()],
        [in_vmem()] * 2,
        [shape_of(prompt_keys.shape, F32), shape_of(prompt_values.shape, F32)],
    )(owned)
    return (*grads, grad_pk, grad_pv)


def solution(mesh):
    in_specs = (
        P(BOTH, None, None),
        P(BOTH, None, None),
        P(BOTH, None, None),
        P(BOTH, None, None),
        P("prompt", "resp", None),
        P("prompt", "resp", None),
        P(),
        P(),
        P(BOTH),
    )
    out_specs = (
        P(BOTH, None, None),
        P(BOTH, None, None),
        P(BOTH, None, None),
        P("prompt", "resp", None),
        P("prompt", "resp", None),
    )
    return jax.shard_map(
        per_device, mesh=mesh, in_specs=in_specs, out_specs=out_specs, check_vma=False
    )
```

```python
import functools
import math

import jax
import jax.numpy as jnp
from jax import lax
from jax.experimental import pallas as pl
from jax.experimental.pallas import tpu as pltpu
from jax.sharding import PartitionSpec as P

KVH = 4
HD = 128
GRP = 8
HEADS = KVH * GRP
DEAD = 1e30
LINES = (13, 7, 3, 4, 6, 11, 0, 2, 5, 8, 10, 15, 1, 9, 12, 14)
FIRST_PLANE = 4
TOK = 256
HALF = 128
PL = 256
ROWS = 16
KVW = KVH * HD
NPROMPT = 8
PAIRS = GRP // 2
UNITS = 2 * PAIRS
LANES = 2 * HALF
SCALING = 1.0 / math.sqrt(HD)
EXP2_SCALE = SCALING * math.log2(math.e)
BF16 = jnp.bfloat16
F32 = jnp.float32
VMEM_LIMIT = 119 * 512 * 1024
SMALL_LIMIT = 4 * 1024 * 1024
PROMPT_LIMIT = 24 * 1024 * 1024
BOTH = ("prompt", "resp")


def contract_last(a, b):
    return lax.dot_general(a, b, (((1,), (1,)), ((), ())), preferred_element_type=F32)


def matmul(a, b):
    return jnp.dot(a, b, preferred_element_type=F32)


def prepare_kernel(
    order, turn,
    keys_hbm, values_hbm, sizes_hbm, slots_hbm, first_ref,
    out_ref, index_ref, sizes_ref, slots_ref, sems,
):
    copies = [
        pltpu.make_async_copy(src, dst, sems.at[i])
        for i, (src, dst) in enumerate(
            (
                (sizes_hbm, sizes_ref),
                (slots_hbm, slots_ref),
                (keys_hbm.at[0], out_ref.at[1]),
                (values_hbm.at[0], out_ref.at[0]),
            )
        )
    ]
    for copy in copies:
        copy.start()
    copies[0].wait()
    copies[1].wait()
    ends = [sizes_ref[0]]
    for p in range(1, NPROMPT - 1):
        ends.append(ends[-1] + sizes_ref[p])
    for j, member in enumerate(order):
        slot = slots_ref[first_ref[0] + member]
        found = jnp.int32(0)
        for end in ends:
            found = found + (slot >= end).astype(jnp.int32)
        found = found + (NPROMPT - turn)
        found = jnp.where(found >= NPROMPT, found - NPROMPT, found)
        index_ref[j] = found + 1 - 2 * (found & 1)
    copies[2].wait()
    copies[3].wait()
    for i in range(2, NPROMPT):
        out_ref[i] = out_ref[i % 2]


def select_kernel(index_ref, blocks_ref, out_ref):
    for j in range(out_ref.shape[0]):
        out_ref[j] = blocks_ref[index_ref[j]]


def sum_kernel(index_ref, terms_ref, out_ref, acc_ref):
    acc_ref[...] = jnp.zeros_like(acc_ref)
    for j in range(terms_ref.shape[0]):
        acc_ref[index_ref[j]] += terms_ref[j].astype(F32)
    out_ref[...] = acc_ref[...].astype(BF16)


def join_kernel(blocks_ref, keys_ref, values_ref):
    for first, out_ref in ((1, keys_ref), (0, values_ref)):
        terms = [blocks_ref[i].astype(F32) for i in range(first, NPROMPT, 2)]
        out_ref[0] = (terms[0] + terms[1]) + (terms[2] + terms[3])


def unit_rows(ref, pair, upper):
    rows = slice(upper * HALF, (upper + 1) * HALF)
    at = pair * 2 * HD
    return jnp.concatenate(
        [ref[0, rows, at : at + HD], ref[0, rows, at + HD : at + 2 * HD]], axis=0
    )


def all_rows(ref):
    return jnp.concatenate(
        [unit_rows(ref, pair, upper) for upper in range(2) for pair in range(PAIRS)], axis=0
    )


def resp_scores(kr, q, upper):
    count = HALF * (1 + upper)
    s = contract_last(kr[:count], q)
    lane = lax.broadcasted_iota(jnp.int32, (HALF, LANES), 1) % HALF
    causal = lax.broadcasted_iota(jnp.int32, (HALF, LANES), 0) <= lane
    last = jnp.where(causal, s[count - HALF :], -1e30)
    if upper:
        return jnp.concatenate([s[:HALF], last], axis=0)
    return last


def resp_stats_kernel(q_ref, do_ref, kr_ref, vr_ref, stats_ref):
    kr = kr_ref[0]
    vr = vr_ref[0]
    for upper in range(2):
        for pair in range(PAIRS):
            q = unit_rows(q_ref, pair, upper)
            do = unit_rows(do_ref, pair, upper)
            s = resp_scores(kr, q, upper)
            d = contract_last(vr[: HALF * (1 + upper)], do)
            m = jnp.max(s, axis=0, keepdims=True)
            e = jnp.exp2(s * EXP2_SCALE - m * EXP2_SCALE)
            total = jnp.sum(e, axis=0, keepdims=True)
            weighted = jnp.sum(e * d, axis=0, keepdims=True)
            rows = slice(upper * HALF, (upper + 1) * HALF)
            for i, value in enumerate((m, total, weighted)):
                stats_ref[2 * pair, i : i + 1, rows] = value[:, :HALF]
                stats_ref[2 * pair + 1, i : i + 1, rows] = value[:, HALF:]


def prompt_kernel(
    length_ref, q_ref, do_ref, kp_ref, vp_ref, stats_ref,
    grad_ref, keys_ref, ds_ref, final_ref, p_ref,
):
    length = length_ref[0]
    kp = kp_ref[0]
    vp = vp_ref[0]
    lane = lax.broadcasted_iota(jnp.int32, (1, TOK), 1)
    heads = [slice(h * HD, (h + 1) * HD) for h in range(GRP)]
    for h in range(GRP):
        q = q_ref[0, :, heads[h]]
        do = do_ref[0, :, heads[h]]
        s = contract_last(kp, q)
        d = contract_last(vp, do)
        resp_m = stats_ref[h, 0:1]
        m = jnp.maximum(jnp.max(s, axis=0, keepdims=True), resp_m)
        e = jnp.exp2(s * EXP2_SCALE - m * EXP2_SCALE)
        fade = jnp.exp2((resp_m - m) * EXP2_SCALE)
        total = jnp.sum(e, axis=0, keepdims=True) + fade * stats_ref[h, 1:2]
        weighted = jnp.sum(e * d, axis=0, keepdims=True) + fade * stats_ref[h, 2:3]
        r = weighted / total
        z = jnp.where(lane < length, m * EXP2_SCALE + jnp.log2(total), DEAD)
        p = jnp.exp2(s * EXP2_SCALE - z)
        cols = slice(h * TOK, (h + 1) * TOK)
        ds_ref[:, cols] = (p * (d - r)).astype(BF16)
        p_ref[:, cols] = p.astype(BF16)
        final_ref[h, 0:1] = z
        final_ref[h, 1:2] = r
    dk = matmul(ds_ref[...], jnp.concatenate([q_ref[0, :, c] for c in heads], axis=0))
    dv = matmul(p_ref[...], jnp.concatenate([do_ref[0, :, c] for c in heads], axis=0))
    grad_ref[0] = dv.astype(BF16)
    grad_ref[1] = (dk * SCALING).astype(BF16)
    keys_ref[...] = kp


def resp_kernel(
    q_ref, do_ref, kr_ref, vr_ref, kp_ref, ds_hbm, final_ref,
    dq_ref, dkr_ref, dvr_ref, dsr_ref, p_ref, ds_ref, sems,
):
    step = pl.program_id(0)
    slot = step % 2

    def load(k):
        cols = pl.ds(pl.multiple_of(k * (GRP * TOK), GRP * TOK), GRP * TOK)
        return pltpu.make_async_copy(ds_hbm.at[:, cols], ds_ref.at[k % 2], sems.at[k % 2])

    @pl.when(step == 0)
    def _():
        load(step).start()

    @pl.when(step < KVH - 1)
    def _():
        load(step + 1).start()

    kr = kr_ref[0]
    vr = vr_ref[0]
    keys_t = jnp.transpose(jnp.concatenate([kp_ref[...], kr], axis=0))
    units = [(upper, pair) for upper in range(2) for pair in range(PAIRS)]
    for unit, (upper, pair) in enumerate(units):
        count = HALF * (1 + upper)
        rows = slice(upper * HALF, (upper + 1) * HALF)
        q = unit_rows(q_ref, pair, upper)
        do = unit_rows(do_ref, pair, upper)
        s = resp_scores(kr, q, upper)
        d = contract_last(vr[:count], do)
        z, r = (
            jnp.concatenate(
                [final_ref[h, i : i + 1, rows] for h in (2 * pair, 2 * pair + 1)], axis=1
            )
            for i in range(2)
        )
        p = jnp.exp2(s * EXP2_SCALE - z)
        cols = slice(unit * LANES, (unit + 1) * LANES)
        dsr_ref[:count, cols] = (p * (d - r)).astype(BF16)
        p_ref[:count, cols] = p.astype(BF16)
    load(step).wait()
    for unit, (upper, pair) in enumerate(units):
        count = HALF * (1 + upper)
        rows = slice(upper * HALF, (upper + 1) * HALF)
        cols = slice(unit * LANES, (unit + 1) * LANES)
        prompt_ds = jnp.concatenate(
            [
                ds_ref[slot, :, h * TOK + upper * HALF : h * TOK + (upper + 1) * HALF]
                for h in (2 * pair, 2 * pair + 1)
            ],
            axis=1,
        )
        both = jnp.concatenate([prompt_ds, dsr_ref[:count, cols]], axis=0)
        dq = (jnp.transpose(matmul(keys_t[:, : PL + count], both)) * SCALING).astype(BF16)
        at = pair * 2 * HD
        dq_ref[0, rows, at : at + HD] = dq[:HALF]
        dq_ref[0, rows, at + HD : at + 2 * HD] = dq[HALF:]
    for out_ref, left_ref, right_ref, scale in (
        (dkr_ref, dsr_ref, q_ref, SCALING),
        (dvr_ref, p_ref, do_ref, 1.0),
    ):
        right = all_rows(right_ref)
        split = PAIRS * LANES
        out_ref[0, :HALF] = (matmul(left_ref[:HALF], right) * scale).astype(BF16)
        out_ref[0, HALF:] = (matmul(left_ref[HALF:, split:], right[split:]) * scale).astype(BF16)


def in_smem():
    return pl.BlockSpec(memory_space=pltpu.SMEM)


def in_vmem():
    return pl.BlockSpec(memory_space=pltpu.VMEM)


def shape_of(shape, dtype):
    return jax.ShapeDtypeStruct(shape, dtype)


def params():
    return pltpu.CompilerParams(vmem_limit_bytes=VMEM_LIMIT)


def small(kernel, name, in_specs, out_spec, out_shape, limit=SMALL_LIMIT):
    return pl.pallas_call(
        kernel,
        in_specs=in_specs,
        out_specs=out_spec,
        out_shape=out_shape,
        compiler_params=pltpu.CompilerParams(vmem_limit_bytes=limit),
        name=name,
    )


def cost(keys, matmuls, heads):
    rows = heads * GRP * TOK
    return pl.CostEstimate(
        flops=2 * matmuls * rows * keys * HD * 2,
        bytes_accessed=heads * (2 << 20),
        transcendentals=rows * keys,
    )


def specs(first):
    wide = pl.BlockSpec((1, TOK, GRP * HD), lambda k: (0, 0, first + k))
    narrow = pl.BlockSpec((1, TOK, HD), lambda k: (0, 0, first + k))
    prompt = pl.BlockSpec((PL, HD), lambda k: (0, first + k))
    stats = pl.BlockSpec((GRP, 8, TOK), lambda k: (first + k, 0, 0))
    ds = pl.BlockSpec((PL, GRP * TOK), lambda k: (0, first + k))
    return wide, narrow, prompt, stats, ds


def resp_stats(queries, grad_out, resp_keys, resp_values):
    wide, narrow, _, stats, _ = specs(0)
    return pl.pallas_call(
        resp_stats_kernel,
        grid=(KVH,),
        in_specs=[wide, wide, narrow, narrow],
        out_specs=stats,
        out_shape=shape_of((HEADS, 8, TOK), F32),
        compiler_params=params(),
        cost_estimate=cost(192, 2, KVH),
        name="resp_stats",
    )(queries, grad_out, resp_keys, resp_values)


def prompt_part(lengths, own, queries, grad_out, stats):
    queries, grad_out, stats = (
        pltpu.with_memory_space_constraint(x, pltpu.HBM) for x in (queries, grad_out, stats)
    )
    wide = pl.BlockSpec((1, TOK, GRP * HD), lambda g: (0, 0, g))
    stat = pl.BlockSpec((GRP, 8, TOK), lambda g: (g, 0, 0))
    return pl.pallas_call(
        prompt_kernel,
        grid=(KVH,),
        in_specs=[
            in_smem(),
            wide,
            wide,
            pl.BlockSpec((1, PL, HD), lambda g: (1, 0, g)),
            pl.BlockSpec((1, PL, HD), lambda g: (0, 0, g)),
            stat,
        ],
        out_specs=[
            pl.BlockSpec((2, PL, HD), lambda g: (0, 0, g)),
            pl.BlockSpec((PL, HD), lambda g: (0, g)),
            pl.BlockSpec((PL, GRP * TOK), lambda g: (0, g)),
            stat,
        ],
        out_shape=[
            pltpu.HBM((2, PL, KVW), BF16),
            pltpu.HBM((PL, KVW), BF16),
            pltpu.HBM((PL, HEADS * TOK), BF16),
            pltpu.HBM((HEADS, 8, TOK), F32),
        ],
        scratch_shapes=[
            pltpu.VMEM((PL, GRP * TOK), BF16),
        ],
        compiler_params=pltpu.CompilerParams(vmem_limit_bytes=PROMPT_LIMIT),
        cost_estimate=cost(256, 4, KVH),
        name="prompt_part",
    )(lengths, queries, grad_out, own, own, stats)


def resp_part(queries, grad_out, resp_keys, resp_values, own_keys, ds, final):
    wide, narrow, prompt, stats, _ = specs(0)
    return pl.pallas_call(
        resp_kernel,
        grid=(KVH,),
        in_specs=[
            wide, wide, narrow, narrow, prompt, pl.BlockSpec(memory_space=pl.ANY), stats,
        ],
        out_specs=[wide, narrow, narrow],
        out_shape=[
            shape_of(queries.shape, BF16),
            shape_of(resp_keys.shape, BF16),
            shape_of(resp_keys.shape, BF16),
        ],
        scratch_shapes=[
            pltpu.VMEM((TOK, UNITS * LANES), BF16),
            pltpu.VMEM((TOK, UNITS * LANES), BF16),
            pltpu.VMEM((2, PL, GRP * TOK), BF16),
            pltpu.SemaphoreType.DMA((2,)),
        ],
        compiler_params=params(),
        cost_estimate=cost(256, 5, KVH),
        name="resp_part",
    )(queries, grad_out, resp_keys, resp_values, own_keys, ds, final)


def per_device(
    queries,
    resp_keys,
    resp_values,
    grad_out,
    prompt_keys,
    prompt_values,
    group_sizes,
    slot_response,
    lengths,
):
    planes = lax.axis_size("prompt")
    lines = lax.axis_size("resp")
    mates = 2 * lines
    slots = slot_response.shape[0]
    order = [c * lines + b for c in (1, 0) for b in LINES]
    groups = [[g * mates + j for j in order] for g in range(planes // 2)]
    turn = FIRST_PLANE
    column = [[(i + turn) % planes ^ 1 for i in range(planes)]]
    first = (lax.axis_index("prompt") // 2 * mates).astype(jnp.int32).reshape(1)

    spread, index = pl.pallas_call(
        functools.partial(prepare_kernel, order, turn),
        in_specs=[pl.BlockSpec(memory_space=pl.ANY)] * 4 + [in_smem()],
        out_specs=[in_vmem(), in_smem()],
        out_shape=[
            pltpu.VMEM((NPROMPT, ROWS, KVW), BF16),
            pltpu.SMEM((mates,), jnp.int32),
        ],
        scratch_shapes=[
            pltpu.SMEM((NPROMPT,), jnp.int32),
            pltpu.SMEM((slots,), jnp.int32),
            pltpu.SemaphoreType.DMA((4,)),
        ],
        compiler_params=pltpu.CompilerParams(vmem_limit_bytes=SMALL_LIMIT),
        name="prepare",
    )(
        *(
            pltpu.with_memory_space_constraint(x, pltpu.HBM)
            for x in (prompt_keys, prompt_values, group_sizes, slot_response)
        ),
        first,
    )
    every = lax.all_to_all(spread, "prompt", 0, 0, axis_index_groups=column)
    chosen = small(
        select_kernel,
        "select",
        [in_smem(), in_vmem()],
        in_vmem(),
        shape_of((mates, ROWS, KVW), BF16),
    )(index, every)
    queries, chosen = lax.optimization_barrier((queries, chosen))
    own = lax.all_to_all(chosen, BOTH, 0, 0, axis_index_groups=groups)
    stats = resp_stats(queries, grad_out, resp_keys, resp_values)
    own = own.reshape(2, PL, KVW)
    grad_p, own_keys, ds, final = prompt_part(lengths, own, queries, grad_out, stats)
    terms = lax.all_to_all(
        grad_p.reshape(mates, ROWS, KVW), BOTH, 0, 0, axis_index_groups=groups
    )
    grads = resp_part(queries, grad_out, resp_keys, resp_values, own_keys, ds, final)
    terms, *grads = lax.optimization_barrier((terms, *grads))
    sums = pl.pallas_call(
        sum_kernel,
        in_specs=[in_smem(), in_vmem()],
        out_specs=in_vmem(),
        out_shape=pltpu.VMEM((NPROMPT, ROWS, KVW), BF16),
        scratch_shapes=[pltpu.VMEM((NPROMPT, ROWS, KVW), F32)],
        compiler_params=pltpu.CompilerParams(vmem_limit_bytes=SMALL_LIMIT),
        name="sum_terms",
    )(index, terms)
    owned = lax.all_to_all(sums, "prompt", 0, 0, axis_index_groups=column)
    grad_pk, grad_pv = small(
        join_kernel,
        "join",
        [in_vmem()],
        [in_vmem()] * 2,
        [shape_of(prompt_keys.shape, F32), shape_of(prompt_values.shape, F32)],
    )(owned)
    return (*grads, grad_pk, grad_pv)


def solution(mesh):
    in_specs = (
        P(BOTH, None, None),
        P(BOTH, None, None),
        P(BOTH, None, None),
        P(BOTH, None, None),
        P("prompt", "resp", None),
        P("prompt", "resp", None),
        P(),
        P(),
        P(BOTH),
    )
    out_specs = (
        P(BOTH, None, None),
        P(BOTH, None, None),
        P(BOTH, None, None),
        P("prompt", "resp", None),
        P("prompt", "resp", None),
    )
    return jax.shard_map(
        per_device, mesh=mesh, in_specs=in_specs, out_specs=out_specs, check_vma=False
    )
```

```python
import functools
import math

import jax
import jax.numpy as jnp
from jax import lax
from jax.experimental import pallas as pl
from jax.experimental.pallas import tpu as pltpu
from jax.sharding import PartitionSpec as P

KVH = 4
HD = 128
GRP = 8
HEADS = KVH * GRP
DEAD = 1e30
LINES = (13, 7, 3, 4, 6, 11, 0, 2, 5, 8, 10, 15, 1, 9, 12, 14)
FIRST_PLANE = 4
TOK = 256
HALF = 128
PL = 256
ROWS = 16
KVW = KVH * HD
NPROMPT = 8
PAIRS = GRP // 2
UNITS = 2 * PAIRS
LANES = 2 * HALF
SCALING = 1.0 / math.sqrt(HD)
EXP2_SCALE = SCALING * math.log2(math.e)
BF16 = jnp.bfloat16
F32 = jnp.float32
VMEM_LIMIT = 119 * 512 * 1024
SMALL_LIMIT = 4 * 1024 * 1024
PROMPT_LIMIT = 24 * 1024 * 1024
BOTH = ("prompt", "resp")


def contract_last(a, b):
    return lax.dot_general(a, b, (((1,), (1,)), ((), ())), preferred_element_type=F32)


def matmul(a, b):
    return jnp.dot(a, b, preferred_element_type=F32)


def prepare_kernel(
    order, turn,
    keys_hbm, values_hbm, sizes_hbm, slots_hbm, first_ref,
    out_ref, index_ref, sizes_ref, slots_ref, sems,
):
    copies = [
        pltpu.make_async_copy(src, dst, sems.at[i])
        for i, (src, dst) in enumerate(
            (
                (sizes_hbm, sizes_ref),
                (slots_hbm, slots_ref),
                (keys_hbm.at[0], out_ref.at[1]),
                (values_hbm.at[0], out_ref.at[0]),
            )
        )
    ]
    for copy in copies:
        copy.start()
    copies[0].wait()
    copies[1].wait()
    ends = [sizes_ref[0]]
    for p in range(1, NPROMPT - 1):
        ends.append(ends[-1] + sizes_ref[p])
    for j, member in enumerate(order):
        slot = slots_ref[first_ref[0] + member]
        found = jnp.int32(0)
        for end in ends:
            found = found + (slot >= end).astype(jnp.int32)
        found = found + (NPROMPT - turn)
        found = jnp.where(found >= NPROMPT, found - NPROMPT, found)
        index_ref[j] = found + 1 - 2 * (found & 1)
    copies[2].wait()
    copies[3].wait()
    for i in range(2, NPROMPT):
        out_ref[i] = out_ref[i % 2]


def select_kernel(index_ref, blocks_ref, out_ref):
    for j in range(out_ref.shape[0]):
        out_ref[j] = blocks_ref[index_ref[j]]


def sum_kernel(index_ref, terms_ref, out_ref, acc_ref):
    acc_ref[...] = jnp.zeros_like(acc_ref)
    for j in range(terms_ref.shape[0]):
        acc_ref[index_ref[j]] += terms_ref[j].astype(F32)
    out_ref[...] = acc_ref[...].astype(BF16)


def join_kernel(blocks_ref, keys_ref, values_ref):
    for first, out_ref in ((1, keys_ref), (0, values_ref)):
        terms = [blocks_ref[i].astype(F32) for i in range(first, NPROMPT, 2)]
        out_ref[0] = (terms[0] + terms[1]) + (terms[2] + terms[3])


def unit_rows(ref, pair, upper):
    rows = slice(upper * HALF, (upper + 1) * HALF)
    at = pair * 2 * HD
    return jnp.concatenate(
        [ref[0, rows, at : at + HD], ref[0, rows, at + HD : at + 2 * HD]], axis=0
    )


def all_rows(ref):
    return jnp.concatenate(
        [unit_rows(ref, pair, upper) for upper in range(2) for pair in range(PAIRS)], axis=0
    )


def resp_scores(kr, q, upper):
    count = HALF * (1 + upper)
    s = contract_last(kr[:count], q)
    lane = lax.broadcasted_iota(jnp.int32, (HALF, LANES), 1) % HALF
    causal = lax.broadcasted_iota(jnp.int32, (HALF, LANES), 0) <= lane
    last = jnp.where(causal, s[count - HALF :], -1e30)
    if upper:
        return jnp.concatenate([s[:HALF], last], axis=0)
    return last


def resp_stats_kernel(q_ref, do_ref, kr_ref, vr_ref, stats_ref):
    kr = kr_ref[0]
    vr = vr_ref[0]
    for upper in range(2):
        for pair in range(PAIRS):
            q = unit_rows(q_ref, pair, upper)
            do = unit_rows(do_ref, pair, upper)
            s = resp_scores(kr, q, upper)
            d = contract_last(vr[: HALF * (1 + upper)], do)
            m = jnp.max(s, axis=0, keepdims=True)
            e = jnp.exp2(s * EXP2_SCALE - m * EXP2_SCALE)
            total = jnp.sum(e, axis=0, keepdims=True)
            weighted = jnp.sum(e * d, axis=0, keepdims=True)
            rows = slice(upper * HALF, (upper + 1) * HALF)
            for i, value in enumerate((m, total, weighted)):
                stats_ref[2 * pair, i : i + 1, rows] = value[:, :HALF]
                stats_ref[2 * pair + 1, i : i + 1, rows] = value[:, HALF:]


def prompt_kernel(
    length_ref, q_ref, do_ref, kp_ref, vp_ref, stats_ref,
    grad_ref, keys_ref, ds_ref, final_ref, p_ref,
):
    length = length_ref[0]
    kp = kp_ref[0]
    vp = vp_ref[0]
    lane = lax.broadcasted_iota(jnp.int32, (1, TOK), 1)
    heads = [slice(h * HD, (h + 1) * HD) for h in range(GRP)]
    for h in range(GRP):
        q = q_ref[0, :, heads[h]]
        do = do_ref[0, :, heads[h]]
        s = contract_last(kp, q)
        d = contract_last(vp, do)
        resp_m = stats_ref[h, 0:1]
        m = jnp.maximum(jnp.max(s, axis=0, keepdims=True), resp_m)
        e = jnp.exp2(s * EXP2_SCALE - m * EXP2_SCALE)
        fade = jnp.exp2((resp_m - m) * EXP2_SCALE)
        total = jnp.sum(e, axis=0, keepdims=True) + fade * stats_ref[h, 1:2]
        weighted = jnp.sum(e * d, axis=0, keepdims=True) + fade * stats_ref[h, 2:3]
        r = weighted / total
        z = jnp.where(lane < length, m * EXP2_SCALE + jnp.log2(total), DEAD)
        p = jnp.exp2(s * EXP2_SCALE - z)
        cols = slice(h * TOK, (h + 1) * TOK)
        ds_ref[:, cols] = (p * (d - r)).astype(BF16)
        p_ref[:, cols] = p.astype(BF16)
        final_ref[h, 0:1] = z
        final_ref[h, 1:2] = r
    dk = matmul(ds_ref[...], jnp.concatenate([q_ref[0, :, c] for c in heads], axis=0))
    dv = matmul(p_ref[...], jnp.concatenate([do_ref[0, :, c] for c in heads], axis=0))
    grad_ref[0] = dv.astype(BF16)
    grad_ref[1] = (dk * SCALING).astype(BF16)
    keys_ref[...] = kp


def resp_kernel(
    q_ref, do_ref, kr_ref, vr_ref, kp_ref, ds_hbm, final_ref,
    dq_ref, dkr_ref, dvr_ref, dsr_ref, p_ref, ds_ref, sems,
):
    step = pl.program_id(0)
    slot = step % 2

    def load(k):
        cols = pl.ds(pl.multiple_of(k * (GRP * TOK), GRP * TOK), GRP * TOK)
        return pltpu.make_async_copy(ds_hbm.at[:, cols], ds_ref.at[k % 2], sems.at[k % 2])

    @pl.when(step == 0)
    def _():
        load(step).start()

    @pl.when(step < KVH - 1)
    def _():
        load(step + 1).start()

    kr = kr_ref[0]
    vr = vr_ref[0]
    keys_t = jnp.transpose(jnp.concatenate([kp_ref[...], kr], axis=0))
    units = [(upper, pair) for upper in range(2) for pair in range(PAIRS)]
    for unit, (upper, pair) in enumerate(units):
        count = HALF * (1 + upper)
        rows = slice(upper * HALF, (upper + 1) * HALF)
        q = unit_rows(q_ref, pair, upper)
        do = unit_rows(do_ref, pair, upper)
        s = resp_scores(kr, q, upper)
        d = contract_last(vr[:count], do)
        z, r = (
            jnp.concatenate(
                [final_ref[h, i : i + 1, rows] for h in (2 * pair, 2 * pair + 1)], axis=1
            )
            for i in range(2)
        )
        p = jnp.exp2(s * EXP2_SCALE - z)
        cols = slice(unit * LANES, (unit + 1) * LANES)
        dsr_ref[:count, cols] = (p * (d - r)).astype(BF16)
        p_ref[:count, cols] = p.astype(BF16)
    load(step).wait()
    for unit, (upper, pair) in enumerate(units):
        count = HALF * (1 + upper)
        rows = slice(upper * HALF, (upper + 1) * HALF)
        cols = slice(unit * LANES, (unit + 1) * LANES)
        prompt_ds = jnp.concatenate(
            [
                ds_ref[slot, :, h * TOK + upper * HALF : h * TOK + (upper + 1) * HALF]
                for h in (2 * pair, 2 * pair + 1)
            ],
            axis=1,
        )
        both = jnp.concatenate([prompt_ds, dsr_ref[:count, cols]], axis=0)
        dq = (jnp.transpose(matmul(keys_t[:, : PL + count], both)) * SCALING).astype(BF16)
        at = pair * 2 * HD
        dq_ref[0, rows, at : at + HD] = dq[:HALF]
        dq_ref[0, rows, at + HD : at + 2 * HD] = dq[HALF:]
    for out_ref, left_ref, right_ref, scale in (
        (dkr_ref, dsr_ref, q_ref, SCALING),
        (dvr_ref, p_ref, do_ref, 1.0),
    ):
        right = all_rows(right_ref)
        split = PAIRS * LANES
        late = matmul(left_ref[:, split:], right[split:])
        early = matmul(left_ref[:HALF, :split], right[:split])
        out_ref[0, :HALF] = ((late[:HALF] + early) * scale).astype(BF16)
        out_ref[0, HALF:] = (late[HALF:] * scale).astype(BF16)


def in_smem():
    return pl.BlockSpec(memory_space=pltpu.SMEM)


def in_vmem():
    return pl.BlockSpec(memory_space=pltpu.VMEM)


def shape_of(shape, dtype):
    return jax.ShapeDtypeStruct(shape, dtype)


def params():
    return pltpu.CompilerParams(vmem_limit_bytes=VMEM_LIMIT)


def small(kernel, name, in_specs, out_spec, out_shape, limit=SMALL_LIMIT):
    return pl.pallas_call(
        kernel,
        in_specs=in_specs,
        out_specs=out_spec,
        out_shape=out_shape,
        compiler_params=pltpu.CompilerParams(vmem_limit_bytes=limit),
        name=name,
    )


def cost(keys, matmuls, heads):
    rows = heads * GRP * TOK
    return pl.CostEstimate(
        flops=2 * matmuls * rows * keys * HD * 2,
        bytes_accessed=heads * (2 << 20),
        transcendentals=rows * keys,
    )


def specs(first):
    wide = pl.BlockSpec((1, TOK, GRP * HD), lambda k: (0, 0, first + k))
    narrow = pl.BlockSpec((1, TOK, HD), lambda k: (0, 0, first + k))
    prompt = pl.BlockSpec((PL, HD), lambda k: (0, first + k))
    stats = pl.BlockSpec((GRP, 8, TOK), lambda k: (first + k, 0, 0))
    ds = pl.BlockSpec((PL, GRP * TOK), lambda k: (0, first + k))
    return wide, narrow, prompt, stats, ds


def resp_stats(queries, grad_out, resp_keys, resp_values):
    wide, narrow, _, stats, _ = specs(0)
    return pl.pallas_call(
        resp_stats_kernel,
        grid=(KVH,),
        in_specs=[wide, wide, narrow, narrow],
        out_specs=stats,
        out_shape=shape_of((HEADS, 8, TOK), F32),
        compiler_params=params(),
        cost_estimate=cost(192, 2, KVH),
        name="resp_stats",
    )(queries, grad_out, resp_keys, resp_values)


def prompt_part(lengths, own, queries, grad_out, stats):
    queries, grad_out, stats = (
        pltpu.with_memory_space_constraint(x, pltpu.HBM) for x in (queries, grad_out, stats)
    )
    wide = pl.BlockSpec((1, TOK, GRP * HD), lambda g: (0, 0, g))
    stat = pl.BlockSpec((GRP, 8, TOK), lambda g: (g, 0, 0))
    return pl.pallas_call(
        prompt_kernel,
        grid=(KVH,),
        in_specs=[
            in_smem(),
            wide,
            wide,
            pl.BlockSpec((1, PL, HD), lambda g: (1, 0, g)),
            pl.BlockSpec((1, PL, HD), lambda g: (0, 0, g)),
            stat,
        ],
        out_specs=[
            pl.BlockSpec((2, PL, HD), lambda g: (0, 0, g)),
            pl.BlockSpec((PL, HD), lambda g: (0, g)),
            pl.BlockSpec((PL, GRP * TOK), lambda g: (0, g)),
            stat,
        ],
        out_shape=[
            pltpu.HBM((2, PL, KVW), BF16),
            pltpu.HBM((PL, KVW), BF16),
            pltpu.HBM((PL, HEADS * TOK), BF16),
            pltpu.HBM((HEADS, 8, TOK), F32),
        ],
        scratch_shapes=[
            pltpu.VMEM((PL, GRP * TOK), BF16),
        ],
        compiler_params=pltpu.CompilerParams(vmem_limit_bytes=PROMPT_LIMIT),
        cost_estimate=cost(256, 4, KVH),
        name="prompt_part",
    )(lengths, queries, grad_out, own, own, stats)


def resp_part(queries, grad_out, resp_keys, resp_values, own_keys, ds, final):
    wide, narrow, prompt, stats, _ = specs(0)
    return pl.pallas_call(
        resp_kernel,
        grid=(KVH,),
        in_specs=[
            wide, wide, narrow, narrow, prompt, pl.BlockSpec(memory_space=pl.ANY), stats,
        ],
        out_specs=[wide, narrow, narrow],
        out_shape=[
            shape_of(queries.shape, BF16),
            shape_of(resp_keys.shape, BF16),
            shape_of(resp_keys.shape, BF16),
        ],
        scratch_shapes=[
            pltpu.VMEM((TOK, UNITS * LANES), BF16),
            pltpu.VMEM((TOK, UNITS * LANES), BF16),
            pltpu.VMEM((2, PL, GRP * TOK), BF16),
            pltpu.SemaphoreType.DMA((2,)),
        ],
        compiler_params=params(),
        cost_estimate=cost(256, 5, KVH),
        name="resp_part",
    )(queries, grad_out, resp_keys, resp_values, own_keys, ds, final)


def per_device(
    queries,
    resp_keys,
    resp_values,
    grad_out,
    prompt_keys,
    prompt_values,
    group_sizes,
    slot_response,
    lengths,
):
    planes = lax.axis_size("prompt")
    lines = lax.axis_size("resp")
    mates = 2 * lines
    slots = slot_response.shape[0]
    order = [c * lines + b for c in (1, 0) for b in LINES]
    groups = [[g * mates + j for j in order] for g in range(planes // 2)]
    turn = FIRST_PLANE
    column = [[(i + turn) % planes ^ 1 for i in range(planes)]]
    first = (lax.axis_index("prompt") // 2 * mates).astype(jnp.int32).reshape(1)

    spread, index = pl.pallas_call(
        functools.partial(prepare_kernel, order, turn),
        in_specs=[pl.BlockSpec(memory_space=pl.ANY)] * 4 + [in_smem()],
        out_specs=[in_vmem(), in_smem()],
        out_shape=[
            pltpu.VMEM((NPROMPT, ROWS, KVW), BF16),
            pltpu.SMEM((mates,), jnp.int32),
        ],
        scratch_shapes=[
            pltpu.SMEM((NPROMPT,), jnp.int32),
            pltpu.SMEM((slots,), jnp.int32),
            pltpu.SemaphoreType.DMA((4,)),
        ],
        compiler_params=pltpu.CompilerParams(vmem_limit_bytes=SMALL_LIMIT),
        name="prepare",
    )(
        *(
            pltpu.with_memory_space_constraint(x, pltpu.HBM)
            for x in (prompt_keys, prompt_values, group_sizes, slot_response)
        ),
        first,
    )
    every = lax.all_to_all(spread, "prompt", 0, 0, axis_index_groups=column)
    chosen = small(
        select_kernel,
        "select",
        [in_smem(), in_vmem()],
        in_vmem(),
        shape_of((mates, ROWS, KVW), BF16),
    )(index, every)
    queries, chosen = lax.optimization_barrier((queries, chosen))
    own = lax.all_to_all(chosen, BOTH, 0, 0, axis_index_groups=groups)
    stats = resp_stats(queries, grad_out, resp_keys, resp_values)
    own = own.reshape(2, PL, KVW)
    grad_p, own_keys, ds, final = prompt_part(lengths, own, queries, grad_out, stats)
    terms = lax.all_to_all(
        grad_p.reshape(mates, ROWS, KVW), BOTH, 0, 0, axis_index_groups=groups
    )
    grads = resp_part(queries, grad_out, resp_keys, resp_values, own_keys, ds, final)
    terms, *grads = lax.optimization_barrier((terms, *grads))
    sums = pl.pallas_call(
        sum_kernel,
        in_specs=[in_smem(), in_vmem()],
        out_specs=in_vmem(),
        out_shape=pltpu.VMEM((NPROMPT, ROWS, KVW), BF16),
        scratch_shapes=[pltpu.VMEM((NPROMPT, ROWS, KVW), F32)],
        compiler_params=pltpu.CompilerParams(vmem_limit_bytes=SMALL_LIMIT),
        name="sum_terms",
    )(index, terms)
    owned = lax.all_to_all(sums, "prompt", 0, 0, axis_index_groups=column)
    grad_pk, grad_pv = small(
        join_kernel,
        "join",
        [in_vmem()],
        [in_vmem()] * 2,
        [shape_of(prompt_keys.shape, F32), shape_of(prompt_values.shape, F32)],
    )(owned)
    return (*grads, grad_pk, grad_pv)


def solution(mesh):
    in_specs = (
        P(BOTH, None, None),
        P(BOTH, None, None),
        P(BOTH, None, None),
        P(BOTH, None, None),
        P("prompt", "resp", None),
        P("prompt", "resp", None),
        P(),
        P(),
        P(BOTH),
    )
    out_specs = (
        P(BOTH, None, None),
        P(BOTH, None, None),
        P(BOTH, None, None),
        P("prompt", "resp", None),
        P("prompt", "resp", None),
    )
    return jax.shard_map(
        per_device, mesh=mesh, in_specs=in_specs, out_specs=out_specs, check_vma=False
    )
```
